32 devices in a mesh: groups: 2 (over x), wide: 16 (over z, y, core).
Axes of the slice: x: 2, y: 2, z: 4, core: 2. Of those that a mesh axis runs over, the one named last changes fastest.
Arguments:
- picture_feature_maps: bfloat16 [256, 10, 10, 1536], P(('groups', 'wide')), parts along dimension 0, may hold values from -6 to 6
- partitioned_filter_tensor: bfloat16 [3, 3, 128, 1536], replicated, may hold values from -0.1875 to 0.1875
- picture_token_layer_scaling: float32 [1536], replicated, may hold values from 0.1 to 1.9
- summary_probes: bfloat16 [64, 1536], replicated, may hold values from -6 to 6
- summary_probe_layer_scaling: float32 [1536], replicated, may hold values from 0.1 to 1.9
- asking_projection_tensor: bfloat16 [1536, 1536], P('wide'), may hold values from -0.15625 to 0.15625
- lookup_projection_tensor: bfloat16 [1536, 1536], P('wide'), may hold values from -0.15625 to 0.15625
- content_projection_tensor: bfloat16 [1536, 1536], P('wide'), may hold values from -0.15625 to 0.15625
- final_projection_tensor: bfloat16 [1536, 1536], P(None, 'wide'), may hold values from -0.15625 to 0.15625
- sharpness_coefficient: float32 [16], replicated, may hold values from 0.5 to 64
Outputs:
- attended: float32 [128, 1536], P('groups'), parts along dimension 0
- new_latents: bfloat16 [128, 1536], P('groups'), parts along dimension 0
The draws below stay inside these ranges and needn't reach their ends.
There are 2 independent parts, one for each index of `groups`. The reference program is written for one: setup_inputs(seed, part) draws one part's arguments, and reference() takes and returns one part's arrays. A program takes and returns all parts, laid end to end along the dimension named above; an argument that names none is the same for every part. Nothing has to cross between parts.
All inputs are finite; a program needn't handle non-finite values.
Results may differ from the reference program's by a relative error of at most 0.004.
The reference program's roundings to bfloat16 on the way (of `activated`, `tok_norm`, `lat_norm` and `attention`) count: a program that leaves them out, or rounds other values in their place, can miss the bound.
Values may be sent and summed in bfloat16 or wider, within the bound.
A program may use at most 128 MiB of HBM per device.

```python
import jax
import jax.numpy as jnp
from jax import lax

D = 1536
GW = 128
FOCUS_CHANNELS = 16
SUMMARY_PROBES = 64
MAP = 10
F_DEV = 8
SUBSPACE_DIM = 96
FRAMES = 128
N_WIDE = 16


def draw_sharpness_coefficient(key, part):
    key_level, key_pick = jax.random.split(jax.random.fold_in(key, 17))
    levels = jax.random.uniform(key_level, (FOCUS_CHANNELS,), jnp.float32)
    chosen = jax.random.randint(key_pick, (), 0, FOCUS_CHANNELS)
    values = 0.5 * jnp.power(5.0, levels)
    highest = 2.5
    return jnp.where(jnp.arange(FOCUS_CHANNELS) == chosen, jnp.float32(highest), values).astype(jnp.float32)


def steps_of(key, shape, shards, least, high):
    def one(axis_at, shards_of):
        draws = jax.random.uniform(jax.random.fold_in(jax.random.fold_in(key, 6), axis_at), (shards_of,), jnp.float32, least / len(shards), high / len(shards))
        return jnp.repeat(jnp.exp(draws), shape[axis_at] // shards_of).reshape((-1,) + (1,) * (len(shape) - axis_at - 1))

    loudness = one(*shards[0])
    for cut in shards[1:]:
        loudness = loudness * one(*cut)
    return loudness


def bell_draw(key, extent, deviation, bound, cuts=(), dtype=jnp.bfloat16):
    result = jax.random.normal(key, extent, jnp.float32) * deviation
    if len(cuts) > 0:
        result = steps_of(key, extent, cuts, -0.22, 0.18) * result
    return jnp.clip(result, min=-bound, max=bound).astype(dtype)


def setup_inputs(seed: int = 0, part: int = 0) -> dict:
    streams_of = jax.random.split(jax.random.key(seed), 11)
    part_splits = jax.random.split(jax.random.fold_in(streams_of[10], part), 11)
    picture_feature_maps = bell_draw(part_splits[0], (FRAMES, MAP, MAP, D), 1.0, 6.0, ((0, 16),))
    partitioned_filter_tensor = bell_draw(streams_of[1], (3, 3, GW, D), (9 * GW) ** -0.5, 0.1875)
    picture_token_layer_scaling = jnp.clip(1.0 + 0.18 * jax.random.normal(streams_of[2], (D,), jnp.float32), 0.1, 1.9)
    summary_probes = bell_draw(streams_of[3], (SUMMARY_PROBES, D), 1.0, 6.0)
    summary_probe_layer_scaling = jnp.clip(1.0 + 0.18 * jax.random.normal(streams_of[4], (D,), jnp.float32), 0.1, 1.9)
    asking_projection_tensor = bell_draw(streams_of[5], (D, D), D ** -0.5, 0.15625, ((0, 16),))
    lookup_projection_tensor = bell_draw(streams_of[6], (D, D), D ** -0.5, 0.15625, ((0, 16),))
    content_projection_tensor = bell_draw(streams_of[7], (D, D), D ** -0.5, 0.15625, ((0, 16),))
    final_projection_tensor = bell_draw(streams_of[8], (D, D), D ** -0.5, 0.15625, ((1, 16),))
    sharpness_coefficient = draw_sharpness_coefficient(jax.random.fold_in(streams_of[10], 71), part)
    return dict(picture_feature_maps=picture_feature_maps, partitioned_filter_tensor=partitioned_filter_tensor, picture_token_layer_scaling=picture_token_layer_scaling, summary_probes=summary_probes, summary_probe_layer_scaling=summary_probe_layer_scaling, asking_projection_tensor=asking_projection_tensor, lookup_projection_tensor=lookup_projection_tensor, content_projection_tensor=content_projection_tensor, final_projection_tensor=final_projection_tensor, sharpness_coefficient=sharpness_coefficient)


RESIDUAL_SCALE = 0.2
EPSILON = 1e-06

def layer_norm(values, gain):
    center = values - lax.optimization_barrier(jnp.mean(values, axis=-1, keepdims=True))
    spread = lax.optimization_barrier(jnp.mean(center * center, axis=-1, keepdims=True))
    return center * lax.rsqrt(spread + EPSILON) * gain

def frame_block(block, partitioned_filter_tensor, picture_token_layer_scaling):
    activated = jax.nn.gelu(block.astype(jnp.float32)).astype(jnp.bfloat16)
    convolved = lax.conv_general_dilated(activated.astype(jnp.float32), partitioned_filter_tensor.astype(jnp.float32), (1, 1), 'SAME', dimension_numbers=('NHWC', 'HWIO', 'NHWC'), feature_group_count=D // GW, precision=lax.Precision.HIGHEST)
    summed = block.astype(jnp.float32) + RESIDUAL_SCALE * convolved
    return layer_norm(summed.reshape(-1, D), picture_token_layer_scaling).astype(jnp.bfloat16)

def reference(picture_feature_maps, partitioned_filter_tensor, picture_token_layer_scaling, summary_probes, summary_probe_layer_scaling, asking_projection_tensor, lookup_projection_tensor, content_projection_tensor, final_projection_tensor, sharpness_coefficient):
    blocks = picture_feature_maps.reshape(N_WIDE, F_DEV, MAP, MAP, D)
    tok_norm = lax.map(lambda block: frame_block(block, partitioned_filter_tensor, picture_token_layer_scaling), blocks).reshape(-1, D)
    lat_norm = layer_norm(summary_probes.astype(jnp.float32), summary_probe_layer_scaling).astype(jnp.bfloat16)
    probe_asking_vectors = jnp.dot(lat_norm, asking_projection_tensor, preferred_element_type=jnp.float32)
    rescaled_similarity_logits = probe_asking_vectors.reshape(SUMMARY_PROBES, FOCUS_CHANNELS, SUBSPACE_DIM) * (sharpness_coefficient / jnp.sqrt(jnp.float32(SUBSPACE_DIM)))[None, :, None]
    source = jnp.concatenate([tok_norm, lat_norm], axis=0)
    key_proj = jnp.dot(source, lookup_projection_tensor, preferred_element_type=jnp.float32).reshape(-1, FOCUS_CHANNELS, SUBSPACE_DIM)
    value_proj = jnp.dot(source, content_projection_tensor, preferred_element_type=jnp.float32).reshape(-1, FOCUS_CHANNELS, SUBSPACE_DIM)
    scores = jnp.einsum('lhd,thd->hlt', rescaled_similarity_logits, key_proj, precision=lax.Precision.HIGHEST)
    row_max = lax.optimization_barrier(jnp.max(scores, axis=-1, keepdims=True))
    weights = jnp.exp(scores - row_max)
    row_sum = lax.optimization_barrier(jnp.sum(weights, axis=-1, keepdims=True))
    weighted = jnp.einsum('hlt,thd->hld', weights, value_proj, precision=lax.Precision.HIGHEST)
    attention = (weighted / row_sum).transpose(1, 0, 2).reshape(SUMMARY_PROBES, D).astype(jnp.bfloat16)
    attended = jnp.dot(attention, final_projection_tensor, preferred_element_type=jnp.float32)
    new_latents = (summary_probes.astype(jnp.float32) + attended).astype(jnp.bfloat16)
    return (attended, new_latents)
```

```python
import functools
import math

import jax
import jax.numpy as jnp
import numpy as np
from jax import lax
from jax.experimental import pallas as pl
from jax.experimental.pallas import tpu as pltpu
from jax.sharding import PartitionSpec as P

RESIDUAL_SCALE = 0.2
EPSILON = 1e-06
LANES = 128
NT = (((1,), (1,)), ((), ()))


def layer_norm(values, gain):
    center = values - jnp.mean(values, axis=-1, keepdims=True)
    spread = jnp.mean(center * center, axis=-1, keepdims=True)
    return center * lax.rsqrt(spread + EPSILON) * gain


def window(head, breadth):
    start = head * breadth // LANES * LANES
    stop = -(-(head + 1) * breadth // LANES) * LANES
    return start, stop - start


def head_mask(head, breadth, shape):
    start, width = window(head, breadth)
    lane = lax.broadcasted_iota(jnp.int32, shape, len(shape) - 1) + start
    return (lane >= head * breadth) & (lane < (head + 1) * breadth)


def halves(values):
    high = values.astype(jnp.bfloat16)
    low = (values - high.astype(jnp.float32)).astype(jnp.bfloat16)
    return high, low


def mixer(
    n, heads, chunks,
    maps_ref, filter_ref, gain_ref, pick_ref, lat_own_ref, lat_slice_ref, probes_ref, sharp_ref,
    wq_ref, wk_ref, wv_ref, wo_ref,
    attended_ref, new_ref,
    gathered, qpart, qcore, qrecv, qall, queries, source, u_high, u_low,
    tail, part, received, att_all, cols_all, wo_wide,
    plain, act, summed,
    z_send, z_recv, far_send, y_send, y_recv, x_send, x_recv, pair_send, pair_recv, d_send, d_recv,
    swap_send, swap_recv, hop_send, hop_recv, head_send, head_recv,
):
    channels = sharp_ref.shape[1]
    breadth = channels // heads
    lats = probes_ref.shape[0]
    rows = lats // n
    shard = wk_ref.shape[0]
    line = n // 4
    chips = n // 2
    cut = channels // chunks
    units = 2 * chunks
    split = n // heads
    few = lats // split
    me = lax.axis_index("wide")
    core = lax.rem(me, 2)
    side = lax.rem(me // 2, 2)
    at = me // 4
    chip = me // 2
    team = lax.axis_index("groups")
    odd = lax.rem(team, 2)
    third = shard // 3
    piece = pl.ds(pl.multiple_of(odd * third, third), 2 * third)
    spare = pl.ds(pl.multiple_of(odd * 2 * third, third), third)
    lacking = pl.ds(pl.multiple_of((1 - odd) * 2 * third, third), third)
    weights = (wk_ref, wv_ref)
    far = line >= 4

    def place(a, b, c):
        return a * 4 + b * 2 + c

    def remote(src, dst, send, recv, target):
        return pltpu.make_async_remote_copy(
            src_ref=src, dst_ref=dst, send_sem=send, recv_sem=recv,
            device_id={"wide": target}, device_id_type=pl.DeviceIdType.MESH,
        )

    def beside(slab, send, recv):
        return pltpu.make_async_remote_copy(
            src_ref=slab, dst_ref=slab, send_sem=send, recv_sem=recv,
            device_id={"groups": team + 1 - 2 * odd, "wide": me},
            device_id_type=pl.DeviceIdType.MESH,
        )

    def each(first, count, body):
        def step(k, carry):
            body(k)
            return carry
        lax.fori_loop(first, count, step, 0)

    def columns(t):
        return t // chunks, pl.ds(pl.multiple_of(lax.rem(t, chunks) * cut, LANES), cut)

    def slab(t, b, a, rows_of):
        w, cols = columns(t)
        return gathered.at[w, core, b, a, rows_of, cols]

    def slabs(t, b, rows_of):
        w, cols = columns(t)
        return gathered.at[w, core, b, :, rows_of, cols]

    def along(t, a):
        own = slab(t, side, at, piece)
        return remote(own, own, z_send.at[t, a], z_recv.at[t, at], place(a, side, core))

    def along_far(t, a):
        block = slab(t, side, a, piece)
        return remote(
            block, block, far_send.at[t], z_recv.at[t, a],
            place(jnp.where(a == 0, line - 1, 0), side, core))

    def across(t, b, a):
        block = slab(t, b, a, piece)
        return remote(
            block, block, y_send.at[t, a], y_recv.at[t, a], place(at, 1 - side, core))

    def aside(t, a, rows_of):
        return beside(slab(t, side, a, rows_of), x_send.at[t, a], x_recv.at[t, a])

    def aside_all(t, rows_of):
        return beside(slabs(t, 1 - side, rows_of), pair_send.at[t], pair_recv.at[t])

    def over(t, c):
        w, cols = columns(t)
        block = gathered.at[w, c, :, :, :, cols]
        return remote(
            block, block, d_send.at[t], d_recv.at[t], place(at, side, 1 - core))

    def direct(a):
        if not far:
            return a != at
        return (a != at) & (jnp.abs(a - at) != line - 1)

    def relays(a):
        if not far:
            return None
        return ((at == line - 2) & (a == 0)) | ((at == 1) & (a == line - 1))

    def nearest(k):
        low = at < (line + 1) // 2
        seen = jnp.where(low, at, line - 1 - at)
        a = jnp.where(k - 1 < seen, k - 1, k)
        return jnp.where(low, a, line - 1 - a)

    def send_own(t):
        def one(k):
            a = nearest(k)

            @pl.when(direct(a))
            def _():
                along(t, a).start()
        each(1, line, one)
        across(t, side, at).start()

    def from_line(t):
        def one(k):
            a = nearest(k)
            own = slab(t, side, a, piece)
            remote(own, own, z_send.at[t, a], z_recv.at[t, a], place(a, side, core)).wait_recv()
            if far:
                @pl.when(relays(a))
                def _():
                    along_far(t, a).start()
            across(t, side, a).start()
            aside(t, a, spare).start()
        each(1, line, one)

    def from_across(t):
        each(0, line, lambda a: across(t, 1 - side, a).wait_recv())
        aside_all(t, spare).start()

    def from_beside(t):
        each(1, line, lambda k: aside(t, nearest(k), lacking).wait_recv())
        aside_all(t, lacking).wait_recv()
        over(t, core).start()

    def advance(t):
        if isinstance(t, int):
            def when(truth, body):
                if truth:
                    body()
        else:
            def when(truth, body):
                pl.when(truth)(body)
        when(t < units, lambda: from_line(t))
        when(t + 2 < units, lambda: send_own(t + 2))
        when((t >= 1) & (t - 1 < units), lambda: from_across(t - 1))
        when((t >= 2) & (t - 2 < units), lambda: from_beside(t - 2))
        when((t >= 3) & (t - 3 < units), lambda: over(t - 3, 1 - core).wait_recv())

    def finish_sends():
        def one(t):
            def two(k):
                a = nearest(k)

                @pl.when(direct(a))
                def _():
                    along(t, a).wait_send()
                if far:
                    @pl.when(relays(a))
                    def _():
                        along_far(t, a).wait_send()
                across(t, side, a).wait_send()
                aside(t, a, spare).wait_send()
            each(1, line, two)
            across(t, side, at).wait_send()
            aside_all(t, spare).wait_send()
            over(t, core).wait_send()
        each(0, units, one)

    def peer(k):
        return lax.rem(chip + k, chips)

    def share(slot, src_of, dst, target, owner):
        return remote(
            src_of(target), dst(owner), swap_send.at[slot, target], swap_recv.at[slot, owner],
            target * 2 + core)

    def share_start(slot, src_of, dst):
        each(1, chips, lambda k: share(slot, src_of, dst, peer(k), chip).start())

    def share_wait(slot, src_of, dst):
        each(1, chips, lambda k: share(slot, src_of, dst, peer(k), chip).wait_send())
        each(1, chips, lambda k: share(slot, src_of, dst, chip, peer(k)).wait_recv())

    def hop(slot, src, dst):
        return remote(
            src, dst, hop_send.at[slot], hop_recv.at[slot], place(at, side, 1 - core))

    def spread_start(slot, everyone):
        mine = everyone.at[core, chip]
        share_start(slot, lambda k: mine, lambda k: everyone.at[core, k])

    def spread_hop(slot, everyone):
        mine = everyone.at[core, chip]
        share_wait(slot, lambda k: mine, lambda k: everyone.at[core, k])
        hop(slot, everyone.at[core], everyone.at[core]).start()

    def spread_wait(slot, everyone):
        hop(slot, everyone.at[core], everyone.at[core]).wait_send()
        hop(slot, everyone.at[1 - core], everyone.at[1 - core]).wait_recv()

    barrier = pltpu.get_barrier_semaphore()
    each(1, n, lambda k: pl.semaphore_signal(
        barrier, inc=1, device_id={"wide": lax.rem(me + k, n)},
        device_id_type=pl.DeviceIdType.MESH))
    pl.semaphore_signal(
        barrier, inc=1, device_id={"groups": team + 1 - 2 * odd, "wide": me},
        device_id_type=pl.DeviceIdType.MESH)
    for w in range(2):
        gathered[w, core, side, at] = weights[w][...]
    pl.semaphore_wait(barrier, n)
    send_own(0)
    partial = jnp.dot(lat_slice_ref[...], wq_ref[...], preferred_element_type=jnp.float32)
    for j in range(n):
        qpart[j // chips, j % chips] = partial[j * rows:(j + 1) * rows]
    hop(3, qpart.at[1 - core], qcore).start()
    send_own(1)

    def q_pair():
        hop(3, qpart.at[1 - core], qcore).wait()
        qpart[core] += qcore[...]
        qrecv[chip] = qpart[core, chip]
        share_start(0, lambda k: qpart.at[core, k], lambda k: qrecv.at[k])

    def q_sum():
        share_wait(0, lambda k: qpart.at[core, k], lambda k: qrecv.at[k])
        qall[core, chip] = jnp.sum(qrecv[...], axis=0) * sharp_ref[...]
        spread_start(1, qall)

    def q_hop():
        spread_hop(1, qall)

    def q_done():
        spread_wait(1, qall)
        for j in range(n):
            queries[j * rows:(j + 1) * rows] = qall[j // chips, j % chips]

    wo_wide[...] = jnp.zeros_like(wo_wide)
    for head in range(heads):
        wo_wide[:, head * LANES:head * LANES + breadth] = (
            wo_ref[:, head * breadth:(head + 1) * breadth])

    frames, high_side, wide_side = maps_ref.shape[:3]
    group = filter_ref.shape[0] // 9
    at_once = plain.shape[0]
    pitch = plain.shape[2]
    flat = high_side * pitch
    steps = frames // at_once
    packed = pick_ref.shape[0]
    real = at_once * high_side * wide_side
    tok_count = steps * packed
    plain[...] = jnp.zeros_like(plain)
    act[...] = jnp.zeros_like(act)
    source[tok_count:] = lat_own_ref[...]

    def convolve(i):
        for f in range(at_once):
            plain[f, :, :wide_side] = maps_ref[i * at_once + f].astype(jnp.float32)
            g = jax.nn.gelu(plain[f]).reshape(flat, channels)
            act[f, 0, pitch:pitch + flat] = pltpu.roll(g, 1, 0).astype(jnp.bfloat16)
            act[f, 1, pitch:pitch + flat] = g.astype(jnp.bfloat16)
            act[f, 2, pitch:pitch + flat] = pltpu.roll(g, flat - 1, 0).astype(jnp.bfloat16)
        for c in range(channels // group):
            cut = slice(c * group, (c + 1) * group)
            taps = jnp.concatenate([
                jnp.concatenate([
                    act[f, dx, dy * pitch:dy * pitch + flat, cut]
                    for dy in range(3) for dx in range(3)
                ], axis=1)
                for f in range(at_once)
            ], axis=0)
            summed[:, cut] = jnp.dot(
                taps, filter_ref[:, cut], preferred_element_type=jnp.float32)
        normed = []
        for f in range(at_once):
            rows_of = slice(f * flat, (f + 1) * flat)
            value = plain[f].reshape(flat, channels) + RESIDUAL_SCALE * summed[rows_of]
            normed.append(layer_norm(value, gain_ref[...]).astype(jnp.bfloat16))
        dense = jnp.dot(
            pick_ref[...], jnp.concatenate(normed, axis=0), preferred_element_type=jnp.float32)
        where = pl.multiple_of(i * packed, 16)
        source[pl.ds(where, packed)] = dense.astype(jnp.bfloat16)

    def conv_and_pass(i):
        convolve(i)
        pl.when(i == 0)(q_pair)
        pl.when(i == 1)(q_sum)
        pl.when(i == 2)(q_hop)
        advance(i)

    each(0, min(steps, 3), conv_and_pass)
    for i in range(min(steps, 3), 3):
        (q_pair, q_sum, q_hop)[i]()
        advance(i)
    for i in range(3, steps):
        convolve(i)
    q_done()
    advance(3)

    per_block = heads // chunks
    lane = lax.broadcasted_iota(jnp.int32, (lats, LANES), 1)

    def weight(w, window_of):
        return jnp.concatenate(
            [gathered[w, j % 2, j // 2 % 2, j // 4, :, window_of] for j in range(n)], axis=0
        ).astype(jnp.bfloat16)

    def attend(first):
        folded = []
        for head in range(first, first + per_block):
            start, width = window(head, breadth)
            part_q = queries[:, start:start + width]
            part_q = jnp.where(head_mask(head, breadth, part_q.shape), part_q, 0.0)
            both = jnp.concatenate(halves(part_q), axis=0)
            look = weight(0, slice(start, start + width))
            raw = lax.dot_general(both, look, NT, preferred_element_type=jnp.float32)
            folded.append(raw[:lats] + raw[lats:])
        high, low = halves(jnp.concatenate(folded, axis=0))
        scores = lax.dot_general(high, source[...], NT, preferred_element_type=jnp.float32)
        scores += lax.dot_general(low, source[...], NT, preferred_element_type=jnp.float32)
        column = lax.broadcasted_iota(jnp.int32, scores.shape, 1)
        live = (column >= tok_count) & (column < tok_count + rows)
        for i in range(steps):
            live |= (column >= i * packed) & (column < i * packed + real)
        scores = jnp.where(live, scores, -jnp.inf)
        row_max = jnp.max(scores, axis=1, keepdims=True)
        terms = jnp.exp(scores - row_max).astype(jnp.bfloat16)
        row_sum = jnp.sum(terms.astype(jnp.float32), axis=1, keepdims=True)
        mixed = jnp.dot(terms, source[...], preferred_element_type=jnp.float32)
        high, low = halves(mixed)
        u_high[first * lats:(first + per_block) * lats] = high
        u_low[first * lats:(first + per_block) * lats] = low
        for i in range(per_block):
            kept = jnp.zeros((lats, LANES), jnp.float32)
            spot = breadth
            for value in (row_max, row_sum):
                rest = value[i * lats:(i + 1) * lats]
                for _ in range(3):
                    top = rest.astype(jnp.bfloat16).astype(jnp.float32)
                    kept = jnp.where(lane == spot, top, kept)
                    rest = rest - top
                    spot += 1
            tail[first + i] = kept

    def project(first):
        for head in range(first, first + per_block):
            start, width = window(head, breadth)
            both = jnp.concatenate(
                [u_high[head * lats:(head + 1) * lats], u_low[head * lats:(head + 1) * lats]],
                axis=0)
            content = weight(1, slice(start, start + width))
            raw = jnp.dot(both, content, preferred_element_type=jnp.float32)
            raw = raw[:lats] + raw[lats:]
            shift = head * breadth - start
            if shift:
                raw = pltpu.roll(raw, width - shift, 1)
            raw = jnp.where(lane < breadth, raw[:, :LANES], tail[head])
            part[head] = raw.astype(jnp.bfloat16)
            for s in range(split):
                to_head(head * split + s, head, s)

    def head_copy(target, head, s, owner):
        return remote(
            part.at[head, s * few:(s + 1) * few], received.at[owner],
            head_send.at[target], head_recv.at[owner], target)

    def to_head(target, head, s):
        @pl.when(me != target)
        def _():
            head_copy(target, head, s, me).start()

        @pl.when(me == target)
        def _():
            received[me] = part[head, s * few:(s + 1) * few]

    for q in range(chunks):
        attend(q * per_block)
        advance(4 + q)
    for q in range(chunks):
        project(q * per_block)
        if q < chunks - 1:
            advance(4 + chunks + q)

    each(1, n, lambda k: head_copy(me, 0, 0, lax.rem(me + k, n)).wait_recv())
    got = received[...].astype(jnp.float32)

    def number(spot):
        return got[:, :, spot:spot + 1] + got[:, :, spot + 1:spot + 2] + got[:, :, spot + 2:spot + 3]

    maxima = number(breadth)
    factor = jnp.exp(maxima - jnp.max(maxima, axis=0, keepdims=True))
    joint = jnp.sum(number(breadth + 3) * factor, axis=0)
    whole = jnp.sum(got * factor, axis=0) / joint
    narrow = lax.broadcasted_iota(jnp.int32, whole.shape, 1) < breadth
    att_all[core, chip] = jnp.where(narrow, whole, 0.0).astype(jnp.bfloat16)
    spread_start(2, att_all)
    spread_hop(2, att_all)
    spread_wait(2, att_all)
    joined = jnp.concatenate([
        jnp.concatenate([
            att_all[(head * split + s) % 2, (head * split + s) // 2] for s in range(split)
        ], axis=0)
        for head in range(heads)
    ], axis=1)
    cols = lax.dot_general(joined, wo_wide[...], NT, preferred_element_type=jnp.float32)
    cols_all[core, chip] = cols.astype(jnp.bfloat16)
    spread_start(4, cols_all)
    spread_hop(4, cols_all)
    spread_wait(4, cols_all)
    wide = wo_ref.shape[0]
    for j in range(n):
        attended_ref[:, j * wide:(j + 1) * wide] = cols_all[j % 2, j // 2].astype(jnp.float32)
    new_ref[...] = (probes_ref[...].astype(jnp.float32) + attended_ref[...]).astype(jnp.bfloat16)
    for target in range(n):
        @pl.when(me != target)
        def _(target=target):
            head_copy(target, target // split, target % split, me).wait_send()
    finish_sends()


def per_device(
    n,
    picture_feature_maps,
    partitioned_filter_tensor,
    picture_token_layer_scaling,
    summary_probes,
    summary_probe_layer_scaling,
    asking_projection_tensor,
    lookup_projection_tensor,
    content_projection_tensor,
    final_projection_tensor,
    sharpness_coefficient,
):
    channels = picture_feature_maps.shape[3]
    heads = sharpness_coefficient.shape[0]
    breadth = channels // heads
    lats = summary_probes.shape[0]
    frames, high_side, wide_side, _ = picture_feature_maps.shape
    at_once = 2 if frames % 2 == 0 else 1
    pitch = -(-(wide_side + 1) // 16) * 16
    flat = high_side * pitch
    real = at_once * high_side * wide_side
    packed = -(-real // 16) * 16
    pick = np.zeros((packed, at_once * flat), np.float32)
    for r in range(real):
        pick[r, r // wide_side * pitch + r % wide_side] = 1.0
    filters = partitioned_filter_tensor.reshape(-1, channels)
    tok_count = frames // at_once * packed
    lat_norm = layer_norm(summary_probes.astype(jnp.float32), summary_probe_layer_scaling).astype(
        jnp.bfloat16
    )
    shard = asking_projection_tensor.shape[0]
    rows = lats // n
    me = lax.axis_index("wide")
    lat_slice = lax.dynamic_slice_in_dim(lat_norm, me * shard, shard, 1)
    lat_own = lax.dynamic_slice_in_dim(lat_norm, me * rows, rows, 0)
    extra = -(-rows // 16) * 16
    lat_own = jnp.pad(lat_own, ((0, extra - rows), (0, 0)))
    sharp = jnp.repeat(sharpness_coefficient / math.sqrt(breadth), breadth)[None, :]
    lookup, content = lookup_projection_tensor, content_projection_tensor
    wire = jnp.bfloat16 if shard % 16 == 0 else jnp.float32
    lookup, content = lookup.astype(wire), content.astype(wire)
    vmem = pl.BlockSpec(memory_space=pltpu.VMEM)
    f32, bf16 = jnp.float32, jnp.bfloat16
    width = final_projection_tensor.shape[1]
    line = n // 4
    chips = n // 2
    chunks = 4
    units = 2 * chunks
    few = lats * heads // n
    return pl.pallas_call(
        functools.partial(mixer, n, heads, chunks),
        out_shape=(
            jax.ShapeDtypeStruct((lats, channels), f32),
            jax.ShapeDtypeStruct((lats, channels), bf16),
        ),
        in_specs=[vmem] * 12,
        out_specs=(vmem, vmem),
        scratch_shapes=[
            pltpu.VMEM((2, 2, 2, line, shard, channels), wire),
            pltpu.VMEM((2, chips, rows, channels), f32),
            pltpu.VMEM((chips, rows, channels), f32),
            pltpu.VMEM((chips, rows, channels), f32),
            pltpu.VMEM((2, chips, rows, channels), f32),
            pltpu.VMEM((lats, channels), f32),
            pltpu.VMEM((tok_count + extra, channels), bf16),
            pltpu.VMEM((heads * lats, channels), bf16),
            pltpu.VMEM((heads * lats, channels), bf16),
            pltpu.VMEM((heads, lats, LANES), f32),
            pltpu.VMEM((heads, lats, LANES), bf16),
            pltpu.VMEM((n, few, LANES), bf16),
            pltpu.VMEM((2, chips, few, LANES), bf16),
            pltpu.VMEM((2, chips, lats, width), bf16),
            pltpu.VMEM((width, heads * LANES), bf16),
            pltpu.VMEM((at_once, high_side, pitch, channels), f32),
            pltpu.VMEM((at_once, 3, flat + 2 * pitch, channels), bf16),
            pltpu.VMEM((at_once * flat, channels), f32),
            pltpu.SemaphoreType.DMA((units, line)),
            pltpu.SemaphoreType.DMA((units, line)),
            pltpu.SemaphoreType.DMA((units,)),
            pltpu.SemaphoreType.DMA((units, line)),
            pltpu.SemaphoreType.DMA((units, line)),
            pltpu.SemaphoreType.DMA((units, line)),
            pltpu.SemaphoreType.DMA((units, line)),
            pltpu.SemaphoreType.DMA((units,)),
            pltpu.SemaphoreType.DMA((units,)),
            pltpu.SemaphoreType.DMA((units,)),
            pltpu.SemaphoreType.DMA((units,)),
            pltpu.SemaphoreType.DMA((5, chips)),
            pltpu.SemaphoreType.DMA((5, chips)),
            pltpu.SemaphoreType.DMA((5,)),
            pltpu.SemaphoreType.DMA((5,)),
            pltpu.SemaphoreType.DMA((n,)),
            pltpu.SemaphoreType.DMA((n,)),
        ],
        compiler_params=pltpu.CompilerParams(
            collective_id=0, has_side_effects=True, vmem_limit_bytes=56 * 1024 * 1024
        ),
    )(
        picture_feature_maps, filters, picture_token_layer_scaling[None, :],
        jnp.asarray(pick, bf16), lat_own, lat_slice, summary_probes, sharp,
        asking_projection_tensor, lookup, content, final_projection_tensor.T,
    )


def solution(mesh):
    placed = (
        P(("groups", "wide"), None, None, None),
        P(),
        P(),
        P(),
        P(),
        P("wide", None),
        P("wide", None),
        P("wide", None),
        P(None, "wide"),
        P(),
    )
    return jax.shard_map(
        functools.partial(per_device, mesh.shape["wide"]),
        mesh=mesh,
        in_specs=placed,
        out_specs=(P("groups", None), P("groups", None)),
        check_vma=False,
    )
```

```python
import functools
import math

import jax
import jax.numpy as jnp
from jax import lax
from jax.experimental import pallas as pl
from jax.experimental.pallas import tpu as pltpu
from jax.sharding import PartitionSpec as P

RESIDUAL_SCALE = 0.2
EPSILON = 1e-06
LANES = 128
AHEAD = 4
NT = (((1,), (1,)), ((), ()))


def layer_norm(values, gain):
    center = values - jnp.mean(values, axis=-1, keepdims=True)
    spread = jnp.mean(center * center, axis=-1, keepdims=True)
    return center * lax.rsqrt(spread + EPSILON) * gain


def window(head, breadth):
    start = head * breadth // LANES * LANES
    stop = -(-(head + 1) * breadth // LANES) * LANES
    return start, stop - start


def head_mask(head, breadth, shape):
    start, width = window(head, breadth)
    lane = lax.broadcasted_iota(jnp.int32, shape, len(shape) - 1) + start
    return (lane >= head * breadth) & (lane < (head + 1) * breadth)


def halves(values):
    high = values.astype(jnp.bfloat16)
    low = (values - high.astype(jnp.float32)).astype(jnp.bfloat16)
    return high, low


def mixer(
    n, heads, chunks,
    maps_hbm, filter_hbm, gain_hbm, probes_hbm, lat_gain_hbm, sharp_ref,
    wq_hbm, wk_hbm, wv_hbm, wo_hbm,
    attended_ref,
    maps_ref, filter_ref, gain_ref, probes_ref, lat_gain_ref, wq_ref, wo_ref,
    row_of, latents, wq_wide, gathered, qpart, qcore, qrecv, qall, queries, source, u_high, u_low,
    tail, part, received, att_all, cols_all, wo_wide,
    act, summed,
    load, own_load, z_send, z_recv, far_send, y_send, y_recv, x_send, x_recv, pair_send, pair_recv, d_send, d_recv,
    swap_send, swap_recv, hop_send, hop_recv, head_send, head_recv,
):
    channels = latents.shape[1]
    breadth = channels // heads
    lats = probes_ref.shape[0]
    rows = lats // n
    shard = wk_hbm.shape[0]
    line = n // 4
    chips = n // 2
    cut = channels // chunks
    units = 2 * chunks
    split = n // heads
    few = lats // split
    me = lax.axis_index("wide")
    core = lax.rem(me, 2)
    side = lax.rem(me // 2, 2)
    at = me // 4
    chip = me // 2
    team = lax.axis_index("groups")
    odd = lax.rem(team, 2)
    third = shard // 3
    piece = pl.ds(pl.multiple_of(odd * third, third), 2 * third)
    spare = pl.ds(pl.multiple_of(odd * 2 * third, third), third)
    lacking = pl.ds(pl.multiple_of((1 - odd) * 2 * third, third), third)
    weights = (wk_hbm, wv_hbm)
    far = line >= 4

    def place(a, b, c):
        return a * 4 + b * 2 + c

    def remote(src, dst, send, recv, target):
        return pltpu.make_async_remote_copy(
            src_ref=src, dst_ref=dst, send_sem=send, recv_sem=recv,
            device_id={"wide": target}, device_id_type=pl.DeviceIdType.MESH,
        )

    def beside(slab, send, recv):
        return pltpu.make_async_remote_copy(
            src_ref=slab, dst_ref=slab, send_sem=send, recv_sem=recv,
            device_id={"groups": team + 1 - 2 * odd, "wide": me},
            device_id_type=pl.DeviceIdType.MESH,
        )

    def each(first, count, body):
        def step(k, carry):
            body(k)
            return carry
        lax.fori_loop(first, count, step, 0)

    def columns(t):
        return t // chunks, pl.ds(pl.multiple_of(lax.rem(t, chunks) * cut, LANES), cut)

    def slab(t, b, a, rows_of):
        w, cols = columns(t)
        return gathered.at[w, core, b, a, rows_of, cols]

    def slabs(t, b, rows_of):
        w, cols = columns(t)
        return gathered.at[w, core, b, :, rows_of, cols]

    def along(t, a):
        own = slab(t, side, at, piece)
        return remote(own, own, z_send.at[t, a], z_recv.at[t, at], place(a, side, core))

    def along_far(t, a):
        block = slab(t, side, a, piece)
        return remote(
            block, block, far_send.at[t], z_recv.at[t, a],
            place(jnp.where(a == 0, line - 1, 0), side, core))

    def across(t, b, a):
        block = slab(t, b, a, piece)
        return remote(
            block, block, y_send.at[t, a], y_recv.at[t, a], place(at, 1 - side, core))

    def aside(t, a, rows_of):
        return beside(slab(t, side, a, rows_of), x_send.at[t, a], x_recv.at[t, a])

    def aside_all(t, rows_of):
        return beside(slabs(t, 1 - side, rows_of), pair_send.at[t], pair_recv.at[t])

    def over(t, c):
        w, cols = columns(t)
        block = gathered.at[w, c, :, :, :, cols]
        return remote(
            block, block, d_send.at[t], d_recv.at[t], place(at, side, 1 - core))

    def direct(a):
        if not far:
            return a != at
        return (a != at) & (jnp.abs(a - at) != line - 1)

    def relays(a):
        if not far:
            return None
        return ((at == line - 2) & (a == 0)) | ((at == 1) & (a == line - 1))

    def nearest(k):
        low = at < (line + 1) // 2
        seen = jnp.where(low, at, line - 1 - at)
        a = jnp.where(k - 1 < seen, k - 1, k)
        return jnp.where(low, a, line - 1 - a)

    def send_own(t):
        def one(k):
            a = nearest(k)

            @pl.when(direct(a))
            def _():
                along(t, a).start()
        each(1, line, one)
        across(t, side, at).start()

    def from_line(t):
        def one(k):
            a = nearest(k)
            own = slab(t, side, a, piece)
            remote(own, own, z_send.at[t, a], z_recv.at[t, a], place(a, side, core)).wait_recv()
            if far:
                @pl.when(relays(a))
                def _():
                    along_far(t, a).start()
            across(t, side, a).start()
            aside(t, a, spare).start()
        each(1, line, one)

    def from_across(t):
        each(0, line, lambda a: across(t, 1 - side, a).wait_recv())
        aside_all(t, spare).start()

    def from_beside(t):
        each(1, line, lambda k: aside(t, nearest(k), lacking).wait_recv())
        aside_all(t, lacking).wait_recv()
        over(t, core).start()

    def advance(t):
        if isinstance(t, int):
            def when(truth, body):
                if truth:
                    body()
        else:
            def when(truth, body):
                pl.when(truth)(body)
        when(t < units, lambda: from_line(t))
        when(t + AHEAD < units, lambda: send_own(t + AHEAD))
        when((t >= 1) & (t - 1 < units), lambda: from_across(t - 1))
        when((t >= 2) & (t - 2 < units), lambda: from_beside(t - 2))
        when((t >= 3) & (t - 3 < units), lambda: over(t - 3, 1 - core).wait_recv())

    def finish_sends():
        def one(t):
            def two(k):
                a = nearest(k)

                @pl.when(direct(a))
                def _():
                    along(t, a).wait_send()
                if far:
                    @pl.when(relays(a))
                    def _():
                        along_far(t, a).wait_send()
                across(t, side, a).wait_send()
                aside(t, a, spare).wait_send()
            each(1, line, two)
            across(t, side, at).wait_send()
            aside_all(t, spare).wait_send()
            over(t, core).wait_send()
        each(0, units, one)

    def peer(k):
        return lax.rem(chip + k, chips)

    def share(slot, src_of, dst, target, owner):
        return remote(
            src_of(target), dst(owner), swap_send.at[slot, target], swap_recv.at[slot, owner],
            target * 2 + core)

    def share_start(slot, src_of, dst):
        each(1, chips, lambda k: share(slot, src_of, dst, peer(k), chip).start())

    def share_wait(slot, src_of, dst):
        each(1, chips, lambda k: share(slot, src_of, dst, peer(k), chip).wait_send())
        each(1, chips, lambda k: share(slot, src_of, dst, chip, peer(k)).wait_recv())

    def hop(slot, src, dst):
        return remote(
            src, dst, hop_send.at[slot], hop_recv.at[slot], place(at, side, 1 - core))

    def spread_start(slot, everyone):
        mine = everyone.at[core, chip]
        share_start(slot, lambda k: mine, lambda k: everyone.at[core, k])

    def spread_hop(slot, everyone):
        mine = everyone.at[core, chip]
        share_wait(slot, lambda k: mine, lambda k: everyone.at[core, k])
        hop(slot, everyone.at[core], everyone.at[core]).start()

    def spread_wait(slot, everyone):
        hop(slot, everyone.at[core], everyone.at[core]).wait_send()
        hop(slot, everyone.at[1 - core], everyone.at[1 - core]).wait_recv()

    taken = [
        pltpu.make_async_copy(src, dst, load.at[k])
        for k, (src, dst) in enumerate((
            (probes_hbm, probes_ref), (lat_gain_hbm, lat_gain_ref), (wq_hbm, wq_ref),
            (maps_hbm, maps_ref), (gain_hbm, gain_ref), (filter_hbm, filter_ref),
            (wo_hbm, wo_ref),
        ))
    ]
    owned = [
        pltpu.make_async_copy(weights[w], gathered.at[w, core, side, at], own_load.at[w])
        for w in range(2)
    ]
    barrier = pltpu.get_barrier_semaphore()
    each(1, n, lambda k: pl.semaphore_signal(
        barrier, inc=1, device_id={"wide": lax.rem(me + k, n)},
        device_id_type=pl.DeviceIdType.MESH))
    pl.semaphore_signal(
        barrier, inc=1, device_id={"groups": team + 1 - 2 * odd, "wide": me},
        device_id_type=pl.DeviceIdType.MESH)
    for copy in owned + taken:
        copy.start()
    lanes_all = lax.broadcasted_iota(jnp.int32, (1, channels), 1)
    sharp = jnp.zeros((1, channels), jnp.float32)
    for head in range(heads):
        inside = (lanes_all >= head * breadth) & (lanes_all < (head + 1) * breadth)
        sharp = jnp.where(inside, sharp_ref[head], sharp)
    row_of[2:3] = sharp / math.sqrt(breadth)
    wq_wide[...] = jnp.zeros_like(wq_wide)
    for copy in taken[:3]:
        copy.wait()
    for k in range(channels // LANES):
        row_of[1:2, k * LANES:(k + 1) * LANES] = lat_gain_ref[k:k + 1]
    latents[...] = layer_norm(
        probes_ref[...].astype(jnp.float32), row_of[1:2]).astype(jnp.bfloat16).astype(jnp.float32)
    deep = wq_wide.shape[0]
    begin = pl.multiple_of(
        jnp.minimum(me * shard // LANES * LANES, channels - deep), LANES)
    wq_wide[pl.ds(pl.multiple_of(me * shard - begin, 8), shard)] = wq_ref[...].astype(jnp.float32)
    partial = jnp.dot(
        latents[:, pl.ds(begin, deep)].astype(jnp.bfloat16), wq_wide[...].astype(jnp.bfloat16),
        preferred_element_type=jnp.float32)
    for j in range(n):
        qpart[j // chips, j % chips] = partial[j * rows:(j + 1) * rows]
    for copy in owned:
        copy.wait()
    pl.semaphore_wait(barrier, n)
    send_own(0)
    hop(3, qpart.at[1 - core], qcore).start()
    for t in range(1, AHEAD):
        send_own(t)

    def q_pair():
        hop(3, qpart.at[1 - core], qcore).wait()
        qpart[core] += qcore[...]
        qrecv[chip] = qpart[core, chip]
        share_start(0, lambda k: qpart.at[core, k], lambda k: qrecv.at[k])

    def q_sum():
        share_wait(0, lambda k: qpart.at[core, k], lambda k: qrecv.at[k])
        qall[core, chip] = jnp.sum(qrecv[...], axis=0) * row_of[2:3]
        spread_start(1, qall)

    def q_hop():
        spread_hop(1, qall)

    def q_done():
        spread_wait(1, qall)
        for j in range(n):
            queries[j * rows:(j + 1) * rows] = qall[j // chips, j % chips]

    pairs = maps_ref.shape[0]
    frames = maps_ref.shape[2]
    high = act.shape[0] - 2
    half = act.shape[1] - 1
    group = filter_ref.shape[0] // 9
    tok_count = pairs * 2 * frames
    first_own = me * rows // 8 * 8

    act[0] = jnp.zeros(act.shape[1:], jnp.bfloat16)
    act[high + 1] = jnp.zeros(act.shape[1:], jnp.bfloat16)
    act[:, 0, 0] = jnp.zeros((high + 2, frames, channels), jnp.bfloat16)
    act[:, half, 1] = jnp.zeros((high + 2, frames, channels), jnp.bfloat16)
    own_rows = latents[pl.ds(pl.multiple_of(first_own, 8), 8)]
    source[tok_count:] = jnp.concatenate(
        [own_rows, jnp.zeros_like(own_rows)], axis=0).astype(jnp.bfloat16)
    taken[3].wait()

    def activate(i):
        g = jax.nn.gelu(maps_ref[i].astype(jnp.float32)).astype(jnp.bfloat16)
        y, p = i // half, lax.rem(i, half)
        act[y + 1, p, 1] = g[0]
        act[y + 1, p + 1, 0] = g[1]

    each(0, pairs, activate)
    taken[4].wait()
    taken[5].wait()
    for k in range(channels // LANES):
        row_of[0:1, k * LANES:(k + 1) * LANES] = gain_ref[k:k + 1]

    def convolve(c):
        lanes = pl.ds(pl.multiple_of(c * group, LANES), group)
        taps = jnp.concatenate([
            act[dy:dy + high, j // 2:j // 2 + half, j % 2, :, lanes].reshape(-1, group)
            for dy in range(3) for j in range(4)
        ], axis=1)
        none = jnp.zeros((group, group), jnp.bfloat16)

        def tap(dy, dx):
            if not 0 <= dx < 3:
                return none
            return filter_ref[(dy * 3 + dx) * group:(dy * 3 + dx + 1) * group, lanes]

        kernel = jnp.concatenate([
            jnp.concatenate([tap(dy, j), tap(dy, j - 1)], axis=1)
            for dy in range(3) for j in range(4)
        ], axis=0)
        both = jnp.dot(taps, kernel, preferred_element_type=jnp.float32)
        both = both.reshape(pairs, frames, 2 * group)
        summed[:, 0, :, lanes] = both[:, :, :group]
        summed[:, 1, :, lanes] = both[:, :, group:]

    def normalize(i):
        value = maps_ref[i].astype(jnp.float32) + RESIDUAL_SCALE * summed[i]
        value = layer_norm(value.reshape(2 * frames, channels), row_of[0:1])
        where = pl.multiple_of(i * 2 * frames, 16)
        source[pl.ds(where, 2 * frames)] = value.astype(jnp.bfloat16)

    parts = channels // group
    each(0, parts // 2, convolve)
    q_pair()
    advance(0)
    each(parts // 2, parts, convolve)
    q_sum()
    advance(1)
    each(0, pairs, normalize)
    q_hop()
    advance(2)
    taken[6].wait()
    wo_wide[...] = jnp.zeros_like(wo_wide)
    for head in range(heads):
        wo_wide[:, head * LANES:head * LANES + breadth] = (
            wo_ref[:, head * breadth:(head + 1) * breadth])
    q_done()
    advance(3)

    per_block = heads // chunks
    lane = lax.broadcasted_iota(jnp.int32, (lats, LANES), 1)

    def weight(w, window_of):
        return jnp.concatenate(
            [gathered[w, j % 2, j // 2 % 2, j // 4, :, window_of] for j in range(n)], axis=0
        ).astype(jnp.bfloat16)

    def attend(first):
        folded = []
        for head in range(first, first + per_block):
            start, width = window(head, breadth)
            part_q = queries[:, start:start + width]
            part_q = jnp.where(head_mask(head, breadth, part_q.shape), part_q, 0.0)
            both = jnp.concatenate(halves(part_q), axis=0)
            look = weight(0, slice(start, start + width))
            raw = lax.dot_general(both, look, NT, preferred_element_type=jnp.float32)
            folded.append(raw[:lats] + raw[lats:])
        high, low = halves(jnp.concatenate(folded, axis=0))
        scores = lax.dot_general(high, source[...], NT, preferred_element_type=jnp.float32)
        scores += lax.dot_general(low, source[...], NT, preferred_element_type=jnp.float32)
        column = lax.broadcasted_iota(jnp.int32, scores.shape, 1)
        own = column - tok_count - (me * rows - first_own)
        live = (column < tok_count) | ((own >= 0) & (own < rows))
        scores = jnp.where(live, scores, -jnp.inf)
        row_max = jnp.max(scores, axis=1, keepdims=True)
        terms = jnp.exp(scores - row_max).astype(jnp.bfloat16)
        row_sum = jnp.sum(terms.astype(jnp.float32), axis=1, keepdims=True)
        mixed = jnp.dot(terms, source[...], preferred_element_type=jnp.float32)
        high, low = halves(mixed)
        u_high[first * lats:(first + per_block) * lats] = high
        u_low[first * lats:(first + per_block) * lats] = low
        for i in range(per_block):
            kept = jnp.zeros((lats, LANES), jnp.float32)
            spot = breadth
            for value in (row_max, row_sum):
                rest = value[i * lats:(i + 1) * lats]
                for _ in range(3):
                    top = rest.astype(jnp.bfloat16).astype(jnp.float32)
                    kept = jnp.where(lane == spot, top, kept)
                    rest = rest - top
                    spot += 1
            tail[first + i] = kept

    def project(first):
        for head in range(first, first + per_block):
            start, width = window(head, breadth)
            both = jnp.concatenate(
                [u_high[head * lats:(head + 1) * lats], u_low[head * lats:(head + 1) * lats]],
                axis=0)
            content = weight(1, slice(start, start + width))
            raw = jnp.dot(both, content, preferred_element_type=jnp.float32)
            raw = raw[:lats] + raw[lats:]
            shift = head * breadth - start
            if shift:
                raw = pltpu.roll(raw, width - shift, 1)
            raw = jnp.where(lane < breadth, raw[:, :LANES], tail[head])
            part[head] = raw.astype(jnp.bfloat16)
            for s in range(split):
                to_head(head * split + s, head, s)

    def head_copy(target, head, s, owner):
        return remote(
            part.at[head, s * few:(s + 1) * few], received.at[owner],
            head_send.at[target], head_recv.at[owner], target)

    def to_head(target, head, s):
        @pl.when(me != target)
        def _():
            head_copy(target, head, s, me).start()

        @pl.when(me == target)
        def _():
            received[me] = part[head, s * few:(s + 1) * few]

    for q in range(chunks):
        attend(q * per_block)
        advance(4 + q)
    for q in range(chunks):
        project(q * per_block)
        if q < chunks - 1:
            advance(4 + chunks + q)

    each(1, n, lambda k: head_copy(me, 0, 0, lax.rem(me + k, n)).wait_recv())
    got = received[...].astype(jnp.float32)

    def number(spot):
        return got[:, :, spot:spot + 1] + got[:, :, spot + 1:spot + 2] + got[:, :, spot + 2:spot + 3]

    maxima = number(breadth)
    factor = jnp.exp(maxima - jnp.max(maxima, axis=0, keepdims=True))
    joint = jnp.sum(number(breadth + 3) * factor, axis=0)
    whole = jnp.sum(got * factor, axis=0) / joint
    narrow = lax.broadcasted_iota(jnp.int32, whole.shape, 1) < breadth
    att_all[core, chip] = jnp.where(narrow, whole, 0.0).astype(jnp.bfloat16)
    spread_start(2, att_all)
    spread_hop(2, att_all)
    spread_wait(2, att_all)
    joined = jnp.concatenate([
        jnp.concatenate([
            att_all[(head * split + s) % 2, (head * split + s) // 2] for s in range(split)
        ], axis=0)
        for head in range(heads)
    ], axis=1)
    cols = lax.dot_general(joined, wo_wide[...], NT, preferred_element_type=jnp.float32)
    cols_all[core, chip] = cols.astype(jnp.bfloat16)
    spread_start(4, cols_all)
    spread_hop(4, cols_all)
    spread_wait(4, cols_all)
    wide = wo_ref.shape[0]
    for j in range(n):
        attended_ref[:, j * wide:(j + 1) * wide] = cols_all[j % 2, j // 2]
    for target in range(n):
        @pl.when(me != target)
        def _(target=target):
            head_copy(target, target // split, target % split, me).wait_send()
    finish_sends()


def per_device(
    n,
    picture_feature_maps,
    partitioned_filter_tensor,
    picture_token_layer_scaling,
    summary_probes,
    summary_probe_layer_scaling,
    asking_projection_tensor,
    lookup_projection_tensor,
    content_projection_tensor,
    final_projection_tensor,
    sharpness_coefficient,
):
    frames, high, across, channels = picture_feature_maps.shape
    heads = sharpness_coefficient.shape[0]
    lats = summary_probes.shape[0]
    maps = picture_feature_maps.transpose(1, 2, 0, 3)
    maps = maps.reshape(high * across // 2, 2, frames, channels)
    filters = partitioned_filter_tensor.reshape(-1, channels)
    tok_count = frames * high * across
    shard = asking_projection_tensor.shape[0]
    rows = lats // n
    extra = 16
    lookup, content = lookup_projection_tensor, content_projection_tensor
    wire = jnp.bfloat16 if shard % 16 == 0 else jnp.float32
    lookup, content = lookup.astype(wire), content.astype(wire)
    anywhere = pl.BlockSpec(memory_space=pl.ANY)
    vmem = pl.BlockSpec(memory_space=pltpu.VMEM)
    smem = pl.BlockSpec(memory_space=pltpu.SMEM)
    f32, bf16 = jnp.float32, jnp.bfloat16
    width = final_projection_tensor.shape[1]
    line = n // 4
    chips = n // 2
    chunks = 4
    units = 2 * chunks
    few = lats * heads // n
    attended = pl.pallas_call(
        functools.partial(mixer, n, heads, chunks),
        out_shape=jax.ShapeDtypeStruct((lats, channels), bf16),
        in_specs=[anywhere] * 5 + [smem] + [anywhere] * 4,
        out_specs=vmem,
        scratch_shapes=[
            pltpu.VMEM(maps.shape, bf16),
            pltpu.VMEM(filters.shape, bf16),
            pltpu.VMEM((channels // LANES, LANES), f32),
            pltpu.VMEM((lats, channels), bf16),
            pltpu.VMEM((channels // LANES, LANES), f32),
            pltpu.VMEM((shard, channels), bf16),
            pltpu.VMEM((width, channels), bf16),
            pltpu.VMEM((8, channels), f32),
            pltpu.VMEM((lats, channels), f32),
            pltpu.VMEM((2 * LANES, channels), f32),
            pltpu.VMEM((2, 2, 2, line, shard, channels), wire),
            pltpu.VMEM((2, chips, rows, channels), f32),
            pltpu.VMEM((chips, rows, channels), f32),
            pltpu.VMEM((chips, rows, channels), f32),
            pltpu.VMEM((2, chips, rows, channels), f32),
            pltpu.VMEM((lats, channels), f32),
            pltpu.VMEM((tok_count + extra, channels), bf16),
            pltpu.VMEM((heads * lats, channels), bf16),
            pltpu.VMEM((heads * lats, channels), bf16),
            pltpu.VMEM((heads, lats, LANES), f32),
            pltpu.VMEM((heads, lats, LANES), bf16),
            pltpu.VMEM((n, few, LANES), bf16),
            pltpu.VMEM((2, chips, few, LANES), bf16),
            pltpu.VMEM((2, chips, lats, width), bf16),
            pltpu.VMEM((width, heads * LANES), bf16),
            pltpu.VMEM((high + 2, across // 2 + 1, 2, frames, channels), bf16),
            pltpu.VMEM((high * across // 2, 2, frames, channels), f32),
            pltpu.SemaphoreType.DMA((7,)),
            pltpu.SemaphoreType.DMA((2,)),
            pltpu.SemaphoreType.DMA((units, line)),
            pltpu.SemaphoreType.DMA((units, line)),
            pltpu.SemaphoreType.DMA((units,)),
            pltpu.SemaphoreType.DMA((units, line)),
            pltpu.SemaphoreType.DMA((units, line)),
            pltpu.SemaphoreType.DMA((units, line)),
            pltpu.SemaphoreType.DMA((units, line)),
            pltpu.SemaphoreType.DMA((units,)),
            pltpu.SemaphoreType.DMA((units,)),
            pltpu.SemaphoreType.DMA((units,)),
            pltpu.SemaphoreType.DMA((units,)),
            pltpu.SemaphoreType.DMA((5, chips)),
            pltpu.SemaphoreType.DMA((5, chips)),
            pltpu.SemaphoreType.DMA((5,)),
            pltpu.SemaphoreType.DMA((5,)),
            pltpu.SemaphoreType.DMA((n,)),
            pltpu.SemaphoreType.DMA((n,)),
        ],
        compiler_params=pltpu.CompilerParams(
            collective_id=0, has_side_effects=True, vmem_limit_bytes=56 * 1024 * 1024
        ),
    )(
        maps, filters, picture_token_layer_scaling.reshape(-1, LANES), summary_probes,
        summary_probe_layer_scaling.reshape(-1, LANES), sharpness_coefficient,
        asking_projection_tensor, lookup, content, final_projection_tensor.T,
    ).astype(f32)
    return attended, (summary_probes.astype(f32) + attended).astype(bf16)


def solution(mesh):
    placed = (
        P(("groups", "wide"), None, None, None),
        P(),
        P(),
        P(),
        P(),
        P("wide", None),
        P("wide", None),
        P("wide", None),
        P(None, "wide"),
        P(),
    )
    return jax.shard_map(
        functools.partial(per_device, mesh.shape["wide"]),
        mesh=mesh,
        in_specs=placed,
        out_specs=(P("groups", None), P("groups", None)),
        check_vma=False,
    )
```

```python
import functools
import math

import jax
import jax.numpy as jnp
from jax import lax
from jax.experimental import pallas as pl
from jax.experimental.pallas import tpu as pltpu
from jax.sharding import PartitionSpec as P

RESIDUAL_SCALE = 0.2
EPSILON = 1e-06
LANES = 128
AHEAD = 3
NT = (((1,), (1,)), ((), ()))


def layer_norm(values, gain):
    center = values - jnp.mean(values, axis=-1, keepdims=True)
    spread = jnp.mean(center * center, axis=-1, keepdims=True)
    return center * lax.rsqrt(spread + EPSILON) * gain


def window(head, breadth):
    start = head * breadth // LANES * LANES
    stop = -(-(head + 1) * breadth // LANES) * LANES
    return start, stop - start


def head_mask(head, breadth, shape):
    start, width = window(head, breadth)
    lane = lax.broadcasted_iota(jnp.int32, shape, len(shape) - 1) + start
    return (lane >= head * breadth) & (lane < (head + 1) * breadth)


def halves(values):
    high = values.astype(jnp.bfloat16)
    low = (values - high.astype(jnp.float32)).astype(jnp.bfloat16)
    return high, low


def mixer(
    n, heads, chunks, blocks,
    maps_hbm, filter_hbm, gain_hbm, probes_hbm, lat_gain_hbm, sharp_ref,
    wq_hbm, wk_hbm, wv_hbm, wo_hbm,
    attended_ref,
    maps_ref, filter_ref, gain_ref, probes_ref, lat_gain_ref, wq_ref, wo_ref,
    row_of, latents, wq_wide, gathered, qpart, qcore, qrecv, qall, queries, source, u_high, u_low,
    tail, part, received, att_all, cols_all, wo_wide,
    act, summed,
    load, own_load, sent, z_recv, y_recv, x_recv, pair_recv, d_recv,
    swap_send, swap_recv, hop_send, hop_recv, head_send, head_recv,
):
    channels = latents.shape[1]
    breadth = channels // heads
    lats = probes_ref.shape[0]
    rows = lats // n
    shard = wk_hbm.shape[0]
    line = n // 4
    chips = n // 2
    cut = channels // chunks
    units = 2 * chunks
    split = n // heads
    few = lats // split
    me = lax.axis_index("wide")
    core = lax.rem(me, 2)
    side = lax.rem(me // 2, 2)
    at = me // 4
    chip = me // 2
    team = lax.axis_index("groups")
    odd = lax.rem(team, 2)
    third = shard // 3
    piece = pl.ds(pl.multiple_of(odd * third, third), 2 * third)
    spare = pl.ds(pl.multiple_of(odd * 2 * third, third), third)
    lacking = pl.ds(pl.multiple_of((1 - odd) * 2 * third, third), third)
    weights = (wk_hbm, wv_hbm)
    assert line >= 4
    far = True

    def place(a, b, c):
        return a * 4 + b * 2 + c

    def remote(src, dst, send, recv, target):
        return pltpu.make_async_remote_copy(
            src_ref=src, dst_ref=dst, send_sem=send, recv_sem=recv,
            device_id={"wide": target}, device_id_type=pl.DeviceIdType.MESH,
        )

    def beside(slab, send, recv):
        return pltpu.make_async_remote_copy(
            src_ref=slab, dst_ref=slab, send_sem=send, recv_sem=recv,
            device_id={"groups": team + 1 - 2 * odd, "wide": me},
            device_id_type=pl.DeviceIdType.MESH,
        )

    def each(first, count, body):
        def step(k, carry):
            body(k)
            return carry
        lax.fori_loop(first, count, step, 0)

    def columns(t):
        return t // chunks, pl.ds(pl.multiple_of(lax.rem(t, chunks) * cut, LANES), cut)

    def slab(t, b, a, rows_of):
        w, cols = columns(t)
        return gathered.at[w, core, b, a, rows_of, cols]

    def slabs(t, b, count, rows_of):
        w, cols = columns(t)
        return gathered.at[w, core, b, :count, rows_of, cols]

    def along(t, a):
        own = slab(t, side, at, piece)
        return remote(own, own, sent.at[0], z_recv.at[t, at], place(a, side, core))

    def along_far(t, a):
        block = slab(t, side, a, piece)
        return remote(
            block, block, sent.at[0], z_recv.at[t, a],
            place(jnp.where(a == 0, line - 1, 0), side, core))

    def over_side(block, recv):
        return remote(block, block, sent.at[1], recv, place(at, 1 - side, core))

    def across_own(b):
        return over_side(gathered.at[:, core, b, at, piece], y_recv.at[units])

    def across(t, a):
        return over_side(slab(t, side, a, piece), y_recv.at[t])

    def aside(t, a):
        return beside(slab(t, side, a, spare), sent.at[2], x_recv.at[t])

    def aside_all(t, rows_of):
        return beside(slabs(t, 1 - side, line, rows_of), sent.at[3], pair_recv.at[t])

    def over(t, c):
        w, cols = columns(t)
        block = gathered.at[w, c, :, :, :, cols]
        return remote(
            block, block, sent.at[4], d_recv.at[t], place(at, side, 1 - core))

    def direct(a):
        if not far:
            return a != at
        return (a != at) & (jnp.abs(a - at) != line - 1)

    def relays(a):
        if not far:
            return None
        return ((at == line - 2) & (a == 0)) | ((at == 1) & (a == line - 1))

    def nearest(k):
        low = at < (line + 1) // 2
        seen = jnp.where(low, at, line - 1 - at)
        a = jnp.where(k - 1 < seen, k - 1, k)
        return jnp.where(low, a, line - 1 - a)

    def send_own(t):
        def one(k):
            a = nearest(k)

            @pl.when(direct(a))
            def _():
                along(t, a).start()
        each(1, line, one)

    def from_line(t):
        def one(k):
            a = nearest(k)
            own = slab(t, side, a, piece)
            remote(own, own, sent.at[0], z_recv.at[t, a], place(a, side, core)).wait_recv()
            if far:
                @pl.when(relays(a))
                def _():
                    along_far(t, a).start()
            across(t, a).start()
            aside(t, a).start()
        each(1, line, one)

    def from_across(t):
        if isinstance(t, int) and t == 0:
            across_own(1 - side).wait_recv()
        over_side(slabs(t, 1 - side, line - 1, piece), y_recv.at[t]).wait_recv()
        aside_all(t, spare).start()

    def from_beside(t):
        beside(slabs(t, side, line - 1, lacking), sent.at[2], x_recv.at[t]).wait_recv()
        aside_all(t, lacking).wait_recv()
        over(t, core).start()

    def advance(t):
        if isinstance(t, int):
            def when(truth, body):
                if truth:
                    body()
        else:
            def when(truth, body):
                pl.when(truth)(body)
        when(t < units, lambda: from_line(t))
        when(t + AHEAD < units, lambda: send_own(t + AHEAD))
        when((t >= 1) & (t - 1 < units), lambda: from_across(t - 1))
        when((t >= 2) & (t - 2 < units), lambda: from_beside(t - 2))
        when((t >= 3) & (t - 3 < units), lambda: over(t - 3, 1 - core).wait_recv())

    def finish_sends():
        def done(k, block):
            remote(block, block, sent.at[k], z_recv.at[0, 0], place(at, side, 1 - core)).wait_send()

        done(0, gathered.at[:, core, side, :line - 2, piece])
        end = (at == 0) | (at == line - 1)
        pl.when(jnp.logical_not(end))(lambda: done(0, gathered.at[:, core, side, 0, piece]))
        pl.when((at == 1) | (at == line - 2))(
            lambda: done(0, gathered.at[:, core, side, 0, piece]))
        done(1, gathered.at[:, core, side, :, piece])
        done(2, gathered.at[:, core, side, :line - 1, spare])
        done(3, gathered.at[:, core, side, :, spare])
        done(4, gathered.at[:, core])

    def peer(k):
        return lax.rem(chip + k, chips)

    def share(slot, src, dst, target):
        return remote(
            src, dst, swap_send.at[slot], swap_recv.at[slot], target * 2 + core)

    def share_start(slot, src_of, dst):
        each(1, chips, lambda k: share(slot, src_of(peer(k)), dst, peer(k)).start())

    def share_wait(slot, most):
        share(slot, most, most, peer(1)).wait_send()
        share(slot, most, most, peer(1)).wait_recv()

    def hop(slot, src, dst):
        return remote(
            src, dst, hop_send.at[slot], hop_recv.at[slot], place(at, side, 1 - core))

    def spread_start(slot, everyone):
        mine = everyone.at[core, chip]
        share_start(slot, lambda k: mine, mine)

    def spread_hop(slot, everyone):
        share_wait(slot, everyone.at[core, :chips - 1])
        hop(slot, everyone.at[core], everyone.at[core]).start()

    def spread_wait(slot, everyone):
        hop(slot, everyone.at[core], everyone.at[core]).wait_send()
        hop(slot, everyone.at[1 - core], everyone.at[1 - core]).wait_recv()

    taken = [
        pltpu.make_async_copy(src, dst, load.at[k])
        for k, (src, dst) in enumerate((
            (probes_hbm, probes_ref), (lat_gain_hbm, lat_gain_ref), (wq_hbm, wq_ref),
            (maps_hbm, maps_ref), (gain_hbm, gain_ref), (filter_hbm, filter_ref),
            (wo_hbm, wo_ref),
        ))
    ]
    owned = [
        pltpu.make_async_copy(weights[w], gathered.at[w, core, side, at], own_load.at[w])
        for w in range(2)
    ]
    barrier = pltpu.get_barrier_semaphore()
    each(1, n, lambda k: pl.semaphore_signal(
        barrier, inc=1, device_id={"wide": lax.rem(me + k, n)},
        device_id_type=pl.DeviceIdType.MESH))
    pl.semaphore_signal(
        barrier, inc=1, device_id={"groups": team + 1 - 2 * odd, "wide": me},
        device_id_type=pl.DeviceIdType.MESH)
    for copy in owned + taken:
        copy.start()
    for copy in owned:
        copy.wait()
    pl.semaphore_wait(barrier, n)
    send_own(0)
    across_own(side).start()
    lanes_all = lax.broadcasted_iota(jnp.int32, (1, channels), 1)
    sharp = jnp.zeros((1, channels), jnp.float32)
    for head in range(heads):
        inside = (lanes_all >= head * breadth) & (lanes_all < (head + 1) * breadth)
        sharp = jnp.where(inside, sharp_ref[head], sharp)
    row_of[2:3] = sharp / math.sqrt(breadth)
    wq_wide[...] = jnp.zeros_like(wq_wide)
    for copy in taken[:3]:
        copy.wait()
    for k in range(channels // LANES):
        row_of[1:2, k * LANES:(k + 1) * LANES] = lat_gain_ref[k:k + 1]
    latents[...] = layer_norm(
        probes_ref[...].astype(jnp.float32), row_of[1:2]).astype(jnp.bfloat16).astype(jnp.float32)
    deep = wq_wide.shape[0]
    begin = pl.multiple_of(
        jnp.minimum(me * shard // LANES * LANES, channels - deep), LANES)
    wq_wide[pl.ds(pl.multiple_of(me * shard - begin, 8), shard)] = wq_ref[...].astype(jnp.float32)
    partial = jnp.dot(
        latents[:, pl.ds(begin, deep)].astype(jnp.bfloat16), wq_wide[...].astype(jnp.bfloat16),
        preferred_element_type=jnp.float32)
    for j in range(n):
        qpart[j // chips, j % chips] = partial[j * rows:(j + 1) * rows]
    hop(3, qpart.at[1 - core], qcore).start()

    def q_pair():
        hop(3, qpart.at[1 - core], qcore).wait()
        qpart[core] += qcore[...]
        qrecv[chip] = qpart[core, chip]
        share_start(0, lambda k: qpart.at[core, k], qrecv.at[chip])

    def q_sum():
        share_wait(0, qrecv.at[:chips - 1])
        qall[core, chip] = jnp.sum(qrecv[...], axis=0) * row_of[2:3]
        spread_start(1, qall)

    def q_hop():
        spread_hop(1, qall)

    def q_done():
        spread_wait(1, qall)
        for j in range(n):
            queries[j * rows:(j + 1) * rows] = qall[j // chips, j % chips]

    pairs = maps_ref.shape[0]
    frames = maps_ref.shape[2]
    high = act.shape[0] - 2
    half = act.shape[1] - 1
    group = filter_ref.shape[0] // 9
    tok_count = pairs * 2 * frames
    first_own = me * rows // 8 * 8

    act[0] = jnp.zeros(act.shape[1:], jnp.bfloat16)
    act[high + 1] = jnp.zeros(act.shape[1:], jnp.bfloat16)
    act[:, 0, 0] = jnp.zeros((high + 2, frames, channels), jnp.bfloat16)
    act[:, half, 1] = jnp.zeros((high + 2, frames, channels), jnp.bfloat16)
    own_rows = latents[pl.ds(pl.multiple_of(first_own, 8), 8)]
    source[tok_count:] = jnp.concatenate(
        [own_rows, jnp.zeros_like(own_rows)], axis=0).astype(jnp.bfloat16)
    q_pair()
    for t in range(1, AHEAD):
        send_own(t)
    taken[3].wait()

    def activate(i):
        g = jax.nn.gelu(maps_ref[i].astype(jnp.float32)).astype(jnp.bfloat16)
        y, p = i // half, lax.rem(i, half)
        act[y + 1, p, 1] = g[0]
        act[y + 1, p + 1, 0] = g[1]

    each(0, pairs, activate)
    taken[4].wait()
    taken[5].wait()
    for k in range(channels // LANES):
        row_of[0:1, k * LANES:(k + 1) * LANES] = gain_ref[k:k + 1]

    def convolve(c):
        lanes = pl.ds(pl.multiple_of(c * group, LANES), group)
        taps = jnp.concatenate([
            act[dy:dy + high, j // 2:j // 2 + half, j % 2, :, lanes].reshape(-1, group)
            for dy in range(3) for j in range(4)
        ], axis=1)
        none = jnp.zeros((group, group), jnp.bfloat16)

        def tap(dy, dx):
            if not 0 <= dx < 3:
                return none
            return filter_ref[(dy * 3 + dx) * group:(dy * 3 + dx + 1) * group, lanes]

        kernel = jnp.concatenate([
            jnp.concatenate([tap(dy, j), tap(dy, j - 1)], axis=1)
            for dy in range(3) for j in range(4)
        ], axis=0)
        both = jnp.dot(taps, kernel, preferred_element_type=jnp.float32)
        both = both.reshape(pairs, frames, 2 * group)
        summed[:, 0, :, lanes] = both[:, :, :group]
        summed[:, 1, :, lanes] = both[:, :, group:]

    def normalize(i):
        value = maps_ref[i].astype(jnp.float32) + RESIDUAL_SCALE * summed[i]
        value = layer_norm(value.reshape(2 * frames, channels), row_of[0:1])
        where = pl.multiple_of(i * 2 * frames, 16)
        source[pl.ds(where, 2 * frames)] = value.astype(jnp.bfloat16)

    parts = channels // group
    together = 5 if pairs % 5 == 0 else 1

    def normalize_some(i):
        for k in range(together):
            normalize(i * together + k)

    advance(0)
    each(0, parts // 2, convolve)
    advance(1)
    q_sum()
    each(parts // 2, parts, convolve)
    advance(2)
    each(0, pairs // together // 2, normalize_some)
    advance(3)
    each(pairs // together // 2, pairs // together, normalize_some)
    taken[6].wait()
    wo_wide[...] = jnp.zeros_like(wo_wide)
    for head in range(heads):
        wo_wide[:, head * LANES:head * LANES + breadth] = (
            wo_ref[:, head * breadth:(head + 1) * breadth])
    q_hop()
    advance(4)
    q_done()

    per_block = heads // blocks
    lane = lax.broadcasted_iota(jnp.int32, (lats, LANES), 1)

    def weight(w, window_of):
        return jnp.concatenate(
            [gathered[w, j % 2, j // 2 % 2, j // 4, :, window_of] for j in range(n)], axis=0
        ).astype(jnp.bfloat16)

    def attend(first):
        folded = []
        for head in range(first, first + per_block):
            start, width = window(head, breadth)
            part_q = queries[:, start:start + width]
            part_q = jnp.where(head_mask(head, breadth, part_q.shape), part_q, 0.0)
            both = jnp.concatenate(halves(part_q), axis=0)
            look = weight(0, slice(start, start + width))
            raw = lax.dot_general(both, look, NT, preferred_element_type=jnp.float32)
            folded.append(raw[:lats] + raw[lats:])
        high, low = halves(jnp.concatenate(folded, axis=0))
        scores = lax.dot_general(high, source[...], NT, preferred_element_type=jnp.float32)
        scores += lax.dot_general(low, source[...], NT, preferred_element_type=jnp.float32)
        column = lax.broadcasted_iota(jnp.int32, scores.shape, 1)
        own = column - tok_count - (me * rows - first_own)
        live = (column < tok_count) | ((own >= 0) & (own < rows))
        scores = jnp.where(live, scores, -jnp.inf)
        row_max = jnp.max(scores, axis=1, keepdims=True)
        terms = jnp.exp(scores - row_max).astype(jnp.bfloat16)
        row_sum = jnp.sum(terms.astype(jnp.float32), axis=1, keepdims=True)
        mixed = jnp.dot(terms, source[...], preferred_element_type=jnp.float32)
        high, low = halves(mixed)
        u_high[first * lats:(first + per_block) * lats] = high
        u_low[first * lats:(first + per_block) * lats] = low
        for i in range(per_block):
            kept = jnp.zeros((lats, LANES), jnp.float32)
            spot = breadth
            for value in (row_max, row_sum):
                rest = value[i * lats:(i + 1) * lats]
                for _ in range(3):
                    top = rest.astype(jnp.bfloat16).astype(jnp.float32)
                    kept = jnp.where(lane == spot, top, kept)
                    rest = rest - top
                    spot += 1
            tail[first + i] = kept

    def project(first):
        for head in range(first, first + per_block):
            start, width = window(head, breadth)
            both = jnp.concatenate(
                [u_high[head * lats:(head + 1) * lats], u_low[head * lats:(head + 1) * lats]],
                axis=0)
            content = weight(1, slice(start, start + width))
            raw = jnp.dot(both, content, preferred_element_type=jnp.float32)
            raw = raw[:lats] + raw[lats:]
            shift = head * breadth - start
            if shift:
                raw = pltpu.roll(raw, width - shift, 1)
            raw = jnp.where(lane < breadth, raw[:, :LANES], tail[head])
            part[head] = raw.astype(jnp.bfloat16)
            for s in range(split):
                to_head(head * split + s, head, s)

    def head_copy(target, head, s, owner):
        return remote(
            part.at[head, s * few:(s + 1) * few], received.at[owner],
            head_send.at[0], head_recv.at[0], target)

    def to_head(target, head, s):
        @pl.when(me != target)
        def _():
            head_copy(target, head, s, me).start()

        @pl.when(me == target)
        def _():
            received[me] = part[head, s * few:(s + 1) * few]

    def ready(q, w):
        return w * chunks + -(-(q + 1) * per_block * breadth // cut) + 2

    step = 5
    for w, work in enumerate((attend, project)):
        for q in range(blocks):
            while step <= ready(q, w):
                advance(step)
                step += 1
            work(q * per_block)
            if w == 0:
                advance(step)
                step += 1

    most = received.at[:n - 1]
    remote(most, most, head_send.at[0], head_recv.at[0], lax.rem(me + 1, n)).wait_recv()
    got = received[...].astype(jnp.float32)

    def number(spot):
        return got[:, :, spot:spot + 1] + got[:, :, spot + 1:spot + 2] + got[:, :, spot + 2:spot + 3]

    maxima = number(breadth)
    factor = jnp.exp(maxima - jnp.max(maxima, axis=0, keepdims=True))
    joint = jnp.sum(number(breadth + 3) * factor, axis=0)
    whole = jnp.sum(got * factor, axis=0) / joint
    narrow = lax.broadcasted_iota(jnp.int32, whole.shape, 1) < breadth
    att_all[core, chip] = jnp.where(narrow, whole, 0.0).astype(jnp.bfloat16)
    spread_start(2, att_all)
    spread_hop(2, att_all)
    spread_wait(2, att_all)
    joined = jnp.concatenate([
        jnp.concatenate([
            att_all[(head * split + s) % 2, (head * split + s) // 2] for s in range(split)
        ], axis=0)
        for head in range(heads)
    ], axis=1)
    cols = lax.dot_general(joined, wo_wide[...], NT, preferred_element_type=jnp.float32)
    cols_all[core, chip] = cols.astype(jnp.bfloat16)
    spread_start(4, cols_all)
    spread_hop(4, cols_all)
    spread_wait(4, cols_all)
    wide = wo_ref.shape[0]
    for j in range(n):
        attended_ref[:, j * wide:(j + 1) * wide] = cols_all[j % 2, j // 2]
    remote(most, most, head_send.at[0], head_recv.at[0], lax.rem(me + 1, n)).wait_send()
    finish_sends()


def per_device(
    n,
    picture_feature_maps,
    partitioned_filter_tensor,
    picture_token_layer_scaling,
    summary_probes,
    summary_probe_layer_scaling,
    asking_projection_tensor,
    lookup_projection_tensor,
    content_projection_tensor,
    final_projection_tensor,
    sharpness_coefficient,
):
    frames, high, across, channels = picture_feature_maps.shape
    heads = sharpness_coefficient.shape[0]
    lats = summary_probes.shape[0]
    maps = picture_feature_maps.transpose(1, 2, 0, 3)
    maps = maps.reshape(high * across // 2, 2, frames, channels)
    filters = partitioned_filter_tensor.reshape(-1, channels)
    tok_count = frames * high * across
    shard = asking_projection_tensor.shape[0]
    rows = lats // n
    extra = 16
    lookup, content = lookup_projection_tensor, content_projection_tensor
    wire = jnp.bfloat16 if shard % 16 == 0 else jnp.float32
    lookup, content = lookup.astype(wire), content.astype(wire)
    anywhere = pl.BlockSpec(memory_space=pl.ANY)
    vmem = pl.BlockSpec(memory_space=pltpu.VMEM)
    smem = pl.BlockSpec(memory_space=pltpu.SMEM)
    f32, bf16 = jnp.float32, jnp.bfloat16
    width = final_projection_tensor.shape[1]
    line = n // 4
    chips = n // 2
    chunks, blocks = 4, 4
    units = 2 * chunks
    few = lats * heads // n
    attended = pl.pallas_call(
        functools.partial(mixer, n, heads, chunks, blocks),
        out_shape=jax.ShapeDtypeStruct((lats, channels), bf16),
        in_specs=[anywhere] * 5 + [smem] + [anywhere] * 4,
        out_specs=vmem,
        scratch_shapes=[
            pltpu.VMEM(maps.shape, bf16),
            pltpu.VMEM(filters.shape, bf16),
            pltpu.VMEM((channels // LANES, LANES), f32),
            pltpu.VMEM((lats, channels), bf16),
            pltpu.VMEM((channels // LANES, LANES), f32),
            pltpu.VMEM((shard, channels), bf16),
            pltpu.VMEM((width, channels), bf16),
            pltpu.VMEM((8, channels), f32),
            pltpu.VMEM((lats, channels), f32),
            pltpu.VMEM((2 * LANES, channels), f32),
            pltpu.VMEM((2, 2, 2, line, shard, channels), wire),
            pltpu.VMEM((2, chips, rows, channels), f32),
            pltpu.VMEM((chips, rows, channels), f32),
            pltpu.VMEM((chips, rows, channels), f32),
            pltpu.VMEM((2, chips, rows, channels), f32),
            pltpu.VMEM((lats, channels), f32),
            pltpu.VMEM((tok_count + extra, channels), bf16),
            pltpu.VMEM((heads * lats, channels), bf16),
            pltpu.VMEM((heads * lats, channels), bf16),
            pltpu.VMEM((heads, lats, LANES), f32),
            pltpu.VMEM((heads, lats, LANES), bf16),
            pltpu.VMEM((n, few, LANES), bf16),
            pltpu.VMEM((2, chips, few, LANES), bf16),
            pltpu.VMEM((2, chips, lats, width), bf16),
            pltpu.VMEM((width, heads * LANES), bf16),
            pltpu.VMEM((high + 2, across // 2 + 1, 2, frames, channels), bf16),
            pltpu.VMEM((high * across // 2, 2, frames, channels), f32),
            pltpu.SemaphoreType.DMA((7,)),
            pltpu.SemaphoreType.DMA((2,)),
            pltpu.SemaphoreType.DMA((5,)),
            pltpu.SemaphoreType.DMA((units, line)),
            pltpu.SemaphoreType.DMA((units + 1,)),
            pltpu.SemaphoreType.DMA((units,)),
            pltpu.SemaphoreType.DMA((units,)),
            pltpu.SemaphoreType.DMA((units,)),
            pltpu.SemaphoreType.DMA((5,)),
            pltpu.SemaphoreType.DMA((5,)),
            pltpu.SemaphoreType.DMA((5,)),
            pltpu.SemaphoreType.DMA((5,)),
            pltpu.SemaphoreType.DMA((1,)),
            pltpu.SemaphoreType.DMA((1,)),
        ],
        compiler_params=pltpu.CompilerParams(
            collective_id=0, has_side_effects=True, vmem_limit_bytes=56 * 1024 * 1024
        ),
    )(
        maps, filters, picture_token_layer_scaling.reshape(-1, LANES), summary_probes,
        summary_probe_layer_scaling.reshape(-1, LANES), sharpness_coefficient,
        asking_projection_tensor, lookup, content, final_projection_tensor.T,
    ).astype(f32)
    return attended, (summary_probes.astype(f32) + attended).astype(bf16)


def solution(mesh):
    placed = (
        P(("groups", "wide"), None, None, None),
        P(),
        P(),
        P(),
        P(),
        P("wide", None),
        P("wide", None),
        P("wide", None),
        P(None, "wide"),
        P(),
    )
    return jax.shard_map(
        functools.partial(per_device, mesh.shape["wide"]),
        mesh=mesh,
        in_specs=placed,
        out_specs=(P("groups", None), P("groups", None)),
        check_vma=False,
    )
```

```python
import functools
import math

import jax
import jax.numpy as jnp
from jax import lax
from jax.experimental import pallas as pl
from jax.experimental.pallas import tpu as pltpu
from jax.sharding import PartitionSpec as P

RESIDUAL_SCALE = 0.2
EPSILON = 1e-06
LANES = 128
AHEAD = 3
NT = (((1,), (1,)), ((), ()))


def layer_norm(values, gain):
    center = values - jnp.mean(values, axis=-1, keepdims=True)
    spread = jnp.mean(center * center, axis=-1, keepdims=True)
    return center * lax.rsqrt(spread + EPSILON) * gain


def window(head, breadth):
    start = head * breadth // LANES * LANES
    stop = -(-(head + 1) * breadth // LANES) * LANES
    return start, stop - start


def head_mask(head, breadth, shape):
    start, width = window(head, breadth)
    lane = lax.broadcasted_iota(jnp.int32, shape, len(shape) - 1) + start
    return (lane >= head * breadth) & (lane < (head + 1) * breadth)


def halves(values):
    high = values.astype(jnp.bfloat16)
    low = (values - high.astype(jnp.float32)).astype(jnp.bfloat16)
    return high, low


def mixer(
    n, heads, chunks, blocks,
    maps_hbm, filter_hbm, gain_hbm, probes_hbm, lat_gain_hbm, sharp_ref,
    wq_hbm, wk_hbm, wv_hbm, wo_hbm,
    attended_ref,
    maps_ref, filter_ref, gain_ref, probes_ref, lat_gain_ref, wq_ref, wo_ref,
    row_of, latents, wq_wide, gathered, qpart, qcore, qrecv, qall, queries, source, u_high, u_low,
    tail, part, received, att_all, cols_all, wo_wide,
    act, summed,
    load, own_load, sent, z_recv, y_recv, x_recv, pair_recv, d_recv,
    swap_send, swap_recv, hop_send, hop_recv, head_send, head_recv,
):
    channels = latents.shape[1]
    breadth = channels // heads
    lats = probes_ref.shape[0]
    rows = lats // n
    shard = wk_hbm.shape[0]
    line = n // 4
    chips = n // 2
    cut = channels // chunks
    units = 2 * chunks
    low_lats = lats // 2
    few = heads * low_lats // chips
    me = lax.axis_index("wide")
    core = lax.rem(me, 2)
    side = lax.rem(me // 2, 2)
    at = me // 4
    chip = me // 2
    team = lax.axis_index("groups")
    odd = lax.rem(team, 2)
    third = shard // 3
    piece = pl.ds(pl.multiple_of(odd * third, third), 2 * third)
    spare = pl.ds(pl.multiple_of(odd * 2 * third, third), third)
    lacking = pl.ds(pl.multiple_of((1 - odd) * 2 * third, third), third)
    weights = (wk_hbm, wv_hbm)
    assert line >= 4
    far = True

    def place(a, b, c):
        return a * 4 + b * 2 + c

    def remote(src, dst, send, recv, target):
        return pltpu.make_async_remote_copy(
            src_ref=src, dst_ref=dst, send_sem=send, recv_sem=recv,
            device_id={"wide": target}, device_id_type=pl.DeviceIdType.MESH,
        )

    def beside(slab, send, recv):
        return pltpu.make_async_remote_copy(
            src_ref=slab, dst_ref=slab, send_sem=send, recv_sem=recv,
            device_id={"groups": team + 1 - 2 * odd, "wide": me},
            device_id_type=pl.DeviceIdType.MESH,
        )

    def each(first, count, body):
        def step(k, carry):
            body(k)
            return carry
        lax.fori_loop(first, count, step, 0)

    def columns(t):
        return t // chunks, pl.ds(pl.multiple_of(lax.rem(t, chunks) * cut, LANES), cut)

    def slab(t, b, a, rows_of):
        w, cols = columns(t)
        return gathered.at[w, core, b, a, rows_of, cols]

    def slabs(t, b, count, rows_of):
        w, cols = columns(t)
        return gathered.at[w, core, b, :count, rows_of, cols]

    def along(t, a):
        own = slab(t, side, at, piece)
        return remote(own, own, sent.at[0], z_recv.at[t, at], place(a, side, core))

    def along_far(t, a):
        block = slab(t, side, a, piece)
        return remote(
            block, block, sent.at[0], z_recv.at[t, a],
            place(jnp.where(a == 0, line - 1, 0), side, core))

    def over_side(block, recv):
        return remote(block, block, sent.at[1], recv, place(at, 1 - side, core))

    def across_own(b):
        return over_side(gathered.at[:, core, b, at, piece], y_recv.at[units])

    def across(t, a):
        return over_side(slab(t, side, a, piece), y_recv.at[t])

    def aside(t, a):
        return beside(slab(t, side, a, spare), sent.at[2], x_recv.at[t])

    def aside_all(t, rows_of):
        return beside(slabs(t, 1 - side, line, rows_of), sent.at[3], pair_recv.at[t])

    def over(t, c):
        w, cols = columns(t)
        block = gathered.at[w, c, :, :, :, cols]
        return remote(
            block, block, sent.at[4], d_recv.at[t], place(at, side, 1 - core))

    def direct(a):
        if not far:
            return a != at
        return (a != at) & (jnp.abs(a - at) != line - 1)

    def relays(a):
        if not far:
            return None
        return ((at == line - 2) & (a == 0)) | ((at == 1) & (a == line - 1))

    def nearest(k):
        low = at < (line + 1) // 2
        seen = jnp.where(low, at, line - 1 - at)
        a = jnp.where(k - 1 < seen, k - 1, k)
        return jnp.where(low, a, line - 1 - a)

    def send_own(t):
        def one(k):
            a = nearest(k)

            @pl.when(direct(a))
            def _():
                along(t, a).start()
        each(1, line, one)

    def from_line(t):
        def one(k):
            a = nearest(k)
            own = slab(t, side, a, piece)
            remote(own, own, sent.at[0], z_recv.at[t, a], place(a, side, core)).wait_recv()
            if far:
                @pl.when(relays(a))
                def _():
                    along_far(t, a).start()
            across(t, a).start()
            aside(t, a).start()
        each(1, line, one)

    def from_across(t):
        if isinstance(t, int) and t == 0:
            across_own(1 - side).wait_recv()
        over_side(slabs(t, 1 - side, line - 1, piece), y_recv.at[t]).wait_recv()
        aside_all(t, spare).start()

    def from_beside(t):
        beside(slabs(t, side, line - 1, lacking), sent.at[2], x_recv.at[t]).wait_recv()
        aside_all(t, lacking).wait_recv()
        over(t, core).start()

    def advance(t):
        if isinstance(t, int):
            def when(truth, body):
                if truth:
                    body()
        else:
            def when(truth, body):
                pl.when(truth)(body)
        when(t < units, lambda: from_line(t))
        when(t + AHEAD < units, lambda: send_own(t + AHEAD))
        when((t >= 1) & (t - 1 < units), lambda: from_across(t - 1))
        when((t >= 2) & (t - 2 < units), lambda: from_beside(t - 2))
        when((t >= 3) & (t - 3 < units), lambda: over(t - 3, 1 - core).wait_recv())

    def finish_sends():
        def done(k, block):
            remote(block, block, sent.at[k], z_recv.at[0, 0], place(at, side, 1 - core)).wait_send()

        done(0, gathered.at[:, core, side, :line - 2, piece])
        end = (at == 0) | (at == line - 1)
        pl.when(jnp.logical_not(end))(lambda: done(0, gathered.at[:, core, side, 0, piece]))
        pl.when((at == 1) | (at == line - 2))(
            lambda: done(0, gathered.at[:, core, side, 0, piece]))
        done(1, gathered.at[:, core, side, :, piece])
        done(2, gathered.at[:, core, side, :line - 1, spare])
        done(3, gathered.at[:, core, side, :, spare])
        done(4, gathered.at[:, core])

    def peer(k):
        return lax.rem(chip + k, chips)

    def share(slot, src, dst, target):
        return remote(
            src, dst, swap_send.at[slot], swap_recv.at[slot], target * 2 + core)

    def share_start(slot, src_of, dst):
        each(1, chips, lambda k: share(slot, src_of(peer(k)), dst, peer(k)).start())

    def share_wait(slot, most):
        share(slot, most, most, peer(1)).wait_send()
        share(slot, most, most, peer(1)).wait_recv()

    def hop(slot, src, dst):
        return remote(
            src, dst, hop_send.at[slot], hop_recv.at[slot], place(at, side, 1 - core))

    def spread_start(slot, everyone):
        mine = everyone.at[core, chip]
        share_start(slot, lambda k: mine, mine)

    def spread_hop(slot, everyone):
        share_wait(slot, everyone.at[core, :chips - 1])
        hop(slot, everyone.at[core], everyone.at[core]).start()

    def spread_wait(slot, everyone):
        hop(slot, everyone.at[core], everyone.at[core]).wait_send()
        hop(slot, everyone.at[1 - core], everyone.at[1 - core]).wait_recv()

    taken = [
        pltpu.make_async_copy(src, dst, load.at[k])
        for k, (src, dst) in enumerate((
            (probes_hbm, probes_ref), (lat_gain_hbm, lat_gain_ref), (wq_hbm, wq_ref),
            (maps_hbm, maps_ref), (gain_hbm, gain_ref), (filter_hbm, filter_ref),
            (wo_hbm, wo_ref.at[core]),
        ))
    ]
    owned = [
        pltpu.make_async_copy(weights[w], gathered.at[w, core, side, at], own_load.at[w])
        for w in range(2)
    ]
    barrier = pltpu.get_barrier_semaphore()
    each(1, n, lambda k: pl.semaphore_signal(
        barrier, inc=1, device_id={"wide": lax.rem(me + k, n)},
        device_id_type=pl.DeviceIdType.MESH))
    pl.semaphore_signal(
        barrier, inc=1, device_id={"groups": team + 1 - 2 * odd, "wide": me},
        device_id_type=pl.DeviceIdType.MESH)
    for copy in owned + taken:
        copy.start()
    for copy in owned:
        copy.wait()
    pl.semaphore_wait(barrier, n)
    send_own(0)
    across_own(side).start()
    lanes_all = lax.broadcasted_iota(jnp.int32, (1, channels), 1)
    sharp = jnp.zeros((1, channels), jnp.float32)
    for head in range(heads):
        inside = (lanes_all >= head * breadth) & (lanes_all < (head + 1) * breadth)
        sharp = jnp.where(inside, sharp_ref[head], sharp)
    row_of[2:3] = sharp / math.sqrt(breadth)
    wq_wide[...] = jnp.zeros_like(wq_wide)
    for copy in taken[:3]:
        copy.wait()
    for k in range(channels // LANES):
        row_of[1:2, k * LANES:(k + 1) * LANES] = lat_gain_ref[k:k + 1]
    latents[...] = layer_norm(
        probes_ref[...].astype(jnp.float32), row_of[1:2]).astype(jnp.bfloat16).astype(jnp.float32)
    deep = wq_wide.shape[0]
    begin = pl.multiple_of(
        jnp.minimum(me * shard // LANES * LANES, channels - deep), LANES)
    wq_wide[pl.ds(pl.multiple_of(me * shard - begin, 8), shard)] = wq_ref[...].astype(jnp.float32)
    partial = jnp.dot(
        latents[:, pl.ds(begin, deep)].astype(jnp.bfloat16), wq_wide[...].astype(jnp.bfloat16),
        preferred_element_type=jnp.float32)
    for j in range(n):
        qpart[j // chips, j % chips] = partial[j * rows:(j + 1) * rows]
    hop(3, qpart.at[1 - core], qcore).start()

    def q_pair():
        hop(3, qpart.at[1 - core], qcore).wait()
        qpart[core] += qcore[...]
        qrecv[chip] = qpart[core, chip]
        share_start(0, lambda k: qpart.at[core, k], qrecv.at[chip])

    def q_sum():
        share_wait(0, qrecv.at[:chips - 1])
        qall[core, chip] = jnp.sum(qrecv[...], axis=0) * row_of[2:3]
        spread_start(1, qall)

    def q_hop():
        spread_hop(1, qall)

    def q_done():
        spread_wait(1, qall)
        for j in range(n):
            queries[j * rows:(j + 1) * rows] = qall[j // chips, j % chips]

    pairs = maps_ref.shape[0]
    frames = maps_ref.shape[2]
    high = act.shape[0] - 2
    half = act.shape[1] - 1
    group = filter_ref.shape[0] // 9
    tok_count = pairs * 2 * frames
    first_own = me * rows // 8 * 8

    act[0] = jnp.zeros(act.shape[1:], jnp.bfloat16)
    act[high + 1] = jnp.zeros(act.shape[1:], jnp.bfloat16)
    act[:, 0, 0] = jnp.zeros((high + 2, frames, channels), jnp.bfloat16)
    act[:, half, 1] = jnp.zeros((high + 2, frames, channels), jnp.bfloat16)
    own_rows = latents[pl.ds(pl.multiple_of(first_own, 8), 8)]
    source[tok_count:] = jnp.concatenate(
        [own_rows, jnp.zeros_like(own_rows)], axis=0).astype(jnp.bfloat16)
    q_pair()
    for t in range(1, AHEAD):
        send_own(t)
    taken[3].wait()

    def activate(i):
        g = jax.nn.gelu(maps_ref[i].astype(jnp.float32)).astype(jnp.bfloat16)
        y, p = i // half, lax.rem(i, half)
        act[y + 1, p, 1] = g[0]
        act[y + 1, p + 1, 0] = g[1]

    each(0, pairs, activate)
    taken[4].wait()
    taken[5].wait()
    for k in range(channels // LANES):
        row_of[0:1, k * LANES:(k + 1) * LANES] = gain_ref[k:k + 1]

    def convolve(c):
        lanes = pl.ds(pl.multiple_of(c * group, LANES), group)
        taps = jnp.concatenate([
            act[dy:dy + high, j // 2:j // 2 + half, j % 2, :, lanes].reshape(-1, group)
            for dy in range(3) for j in range(4)
        ], axis=1)
        none = jnp.zeros((group, group), jnp.bfloat16)

        def tap(dy, dx):
            if not 0 <= dx < 3:
                return none
            return filter_ref[(dy * 3 + dx) * group:(dy * 3 + dx + 1) * group, lanes]

        kernel = jnp.concatenate([
            jnp.concatenate([tap(dy, j), tap(dy, j - 1)], axis=1)
            for dy in range(3) for j in range(4)
        ], axis=0)
        both = jnp.dot(taps, kernel, preferred_element_type=jnp.float32)
        both = both.reshape(pairs, frames, 2 * group)
        summed[:, 0, :, lanes] = both[:, :, :group]
        summed[:, 1, :, lanes] = both[:, :, group:]

    def normalize(i):
        value = maps_ref[i].astype(jnp.float32) + RESIDUAL_SCALE * summed[i]
        value = layer_norm(value.reshape(2 * frames, channels), row_of[0:1])
        where = pl.multiple_of(i * 2 * frames, 16)
        source[pl.ds(where, 2 * frames)] = value.astype(jnp.bfloat16)

    parts = channels // group
    together = 5 if pairs % 5 == 0 else 1

    def normalize_some(i):
        for k in range(together):
            normalize(i * together + k)

    advance(0)
    each(0, parts // 2, convolve)
    taken[6].wait()
    hop(2, wo_ref.at[core], wo_ref.at[core]).start()
    advance(1)
    q_sum()
    each(parts // 2, parts, convolve)
    advance(2)
    each(0, pairs // together // 2, normalize_some)
    advance(3)
    each(pairs // together // 2, pairs // together, normalize_some)
    spread_wait(2, wo_ref)
    wo_wide[...] = jnp.zeros_like(wo_wide)
    for c in range(2):
        for head in range(heads):
            wo_wide[c, :, head * LANES:head * LANES + breadth] = (
                wo_ref[c, :, head * breadth:(head + 1) * breadth])
    q_hop()
    advance(4)
    q_done()

    per_block = heads // blocks
    lane = lax.broadcasted_iota(jnp.int32, (lats, LANES), 1)

    def weight(w, window_of):
        return jnp.concatenate(
            [gathered[w, j % 2, j // 2 % 2, j // 4, :, window_of] for j in range(n)], axis=0
        ).astype(jnp.bfloat16)

    def attend(first):
        folded = []
        for head in range(first, first + per_block):
            start, width = window(head, breadth)
            part_q = queries[:, start:start + width]
            part_q = jnp.where(head_mask(head, breadth, part_q.shape), part_q, 0.0)
            both = jnp.concatenate(halves(part_q), axis=0)
            look = weight(0, slice(start, start + width))
            raw = lax.dot_general(both, look, NT, preferred_element_type=jnp.float32)
            folded.append(raw[:lats] + raw[lats:])
        high, low = halves(jnp.concatenate(folded, axis=0))
        scores = lax.dot_general(high, source[...], NT, preferred_element_type=jnp.float32)
        scores += lax.dot_general(low, source[...], NT, preferred_element_type=jnp.float32)
        column = lax.broadcasted_iota(jnp.int32, scores.shape, 1)
        own = column - tok_count - (me * rows - first_own)
        live = (column < tok_count) | ((own >= 0) & (own < rows))
        scores = jnp.where(live, scores, -jnp.inf)
        row_max = jnp.max(scores, axis=1, keepdims=True)
        terms = jnp.exp(scores - row_max).astype(jnp.bfloat16)
        row_sum = jnp.sum(terms.astype(jnp.float32), axis=1, keepdims=True)
        mixed = jnp.dot(terms, source[...], preferred_element_type=jnp.float32)
        high, low = halves(mixed)
        u_high[first * lats:(first + per_block) * lats] = high
        u_low[first * lats:(first + per_block) * lats] = low
        for i in range(per_block):
            kept = jnp.zeros((lats, LANES), jnp.float32)
            spot = breadth
            for value in (row_max, row_sum):
                rest = value[i * lats:(i + 1) * lats]
                for _ in range(3):
                    top = rest.astype(jnp.bfloat16).astype(jnp.float32)
                    kept = jnp.where(lane == spot, top, kept)
                    rest = rest - top
                    spot += 1
            tail[first + i] = kept

    def project(first):
        for head in range(first, first + per_block):
            start, width = window(head, breadth)
            both = jnp.concatenate(
                [u_high[head * lats:(head + 1) * lats], u_low[head * lats:(head + 1) * lats]],
                axis=0)
            content = weight(1, slice(start, start + width))
            raw = jnp.dot(both, content, preferred_element_type=jnp.float32)
            raw = raw[:lats] + raw[lats:]
            shift = head * breadth - start
            if shift:
                raw = pltpu.roll(raw, width - shift, 1)
            raw = jnp.where(lane < breadth, raw[:, :LANES], tail[head])
            raw = raw.astype(jnp.bfloat16)
            for c in range(2):
                part[c, head * low_lats:(head + 1) * low_lats] = (
                    raw[c * low_lats:(c + 1) * low_lats])
            for k in range(head * low_lats // few, (head + 1) * low_lats // few):
                for c in range(2):
                    to_owner(k, c)

    def to_owner(k, c):
        own = part.at[c, k * few:(k + 1) * few]

        @pl.when(me != k * 2 + c)
        def _():
            remote(own, received.at[me], head_send.at[0], head_recv.at[0], k * 2 + c).start()

        @pl.when(me == k * 2 + c)
        def _():
            received[me] = part[c, k * few:(k + 1) * few]

    def ready(q, w):
        return w * chunks + -(-(q + 1) * per_block * breadth // cut) + 2

    step = 5
    for w, work in enumerate((attend, project)):
        for q in range(blocks):
            while step <= ready(q, w):
                advance(step)
                step += 1
            work(q * per_block)
            if w == 0:
                advance(step)
                step += 1

    most = received.at[:n - 1]
    remote(most, most, head_send.at[0], head_recv.at[0], lax.rem(me + 1, n)).wait_recv()
    got = received[...].astype(jnp.float32)

    def number(spot):
        return got[:, :, spot:spot + 1] + got[:, :, spot + 1:spot + 2] + got[:, :, spot + 2:spot + 3]

    maxima = number(breadth)
    factor = jnp.exp(maxima - jnp.max(maxima, axis=0, keepdims=True))
    joint = jnp.sum(number(breadth + 3) * factor, axis=0)
    whole = jnp.sum(got * factor, axis=0) / joint
    narrow = lax.broadcasted_iota(jnp.int32, whole.shape, 1) < breadth
    att_all[chip] = jnp.where(narrow, whole, 0.0).astype(jnp.bfloat16)
    mine = att_all.at[chip]
    share_start(2, lambda k: mine, mine)
    share_wait(2, att_all.at[:chips - 1])
    pieces = low_lats // few if few < low_lats else 1
    heads_at = few // low_lats if few > low_lats else 1
    joined = []
    for head in range(heads):
        if few >= low_lats:
            first = head % heads_at * low_lats
            joined.append(att_all[head // heads_at, first:first + low_lats])
        else:
            joined.append(jnp.concatenate(
                [att_all[head * pieces + i] for i in range(pieces)], axis=0))
    joined = jnp.concatenate(joined, axis=1)
    wide = wo_ref.shape[1]
    for c in range(2):
        cols = lax.dot_general(joined, wo_wide[c], NT, preferred_element_type=jnp.float32)
        cols_all[core, chip, :, c * wide:(c + 1) * wide] = cols.astype(jnp.bfloat16)
    spread_start(4, cols_all)
    spread_hop(4, cols_all)
    spread_wait(4, cols_all)
    for c in range(2):
        for k in range(chips):
            attended_ref[c * low_lats:(c + 1) * low_lats, k * 2 * wide:(k + 1) * 2 * wide] = (
                cols_all[c, k])
    remote(most, most, head_send.at[0], head_recv.at[0], lax.rem(me + 1, n)).wait_send()
    finish_sends()


def per_device(
    n,
    picture_feature_maps,
    partitioned_filter_tensor,
    picture_token_layer_scaling,
    summary_probes,
    summary_probe_layer_scaling,
    asking_projection_tensor,
    lookup_projection_tensor,
    content_projection_tensor,
    final_projection_tensor,
    sharpness_coefficient,
):
    frames, high, across, channels = picture_feature_maps.shape
    heads = sharpness_coefficient.shape[0]
    lats = summary_probes.shape[0]
    maps = picture_feature_maps.transpose(1, 2, 0, 3)
    maps = maps.reshape(high * across // 2, 2, frames, channels)
    filters = partitioned_filter_tensor.reshape(-1, channels)
    tok_count = frames * high * across
    shard = asking_projection_tensor.shape[0]
    rows = lats // n
    extra = 16
    lookup, content = lookup_projection_tensor, content_projection_tensor
    wire = jnp.bfloat16 if shard % 16 == 0 else jnp.float32
    lookup, content = lookup.astype(wire), content.astype(wire)
    anywhere = pl.BlockSpec(memory_space=pl.ANY)
    vmem = pl.BlockSpec(memory_space=pltpu.VMEM)
    smem = pl.BlockSpec(memory_space=pltpu.SMEM)
    f32, bf16 = jnp.float32, jnp.bfloat16
    width = final_projection_tensor.shape[1]
    line = n // 4
    chips = n // 2
    chunks, blocks = 4, 4
    units = 2 * chunks
    few = lats * heads // n
    attended = pl.pallas_call(
        functools.partial(mixer, n, heads, chunks, blocks),
        out_shape=jax.ShapeDtypeStruct((lats, channels), bf16),
        in_specs=[anywhere] * 5 + [smem] + [anywhere] * 4,
        out_specs=vmem,
        scratch_shapes=[
            pltpu.VMEM(maps.shape, bf16),
            pltpu.VMEM(filters.shape, bf16),
            pltpu.VMEM((channels // LANES, LANES), f32),
            pltpu.VMEM((lats, channels), bf16),
            pltpu.VMEM((channels // LANES, LANES), f32),
            pltpu.VMEM((shard, channels), bf16),
            pltpu.VMEM((2, width, channels), bf16),
            pltpu.VMEM((8, channels), f32),
            pltpu.VMEM((lats, channels), f32),
            pltpu.VMEM((2 * LANES, channels), f32),
            pltpu.VMEM((2, 2, 2, line, shard, channels), wire),
            pltpu.VMEM((2, chips, rows, channels), f32),
            pltpu.VMEM((chips, rows, channels), f32),
            pltpu.VMEM((chips, rows, channels), f32),
            pltpu.VMEM((2, chips, rows, channels), f32),
            pltpu.VMEM((lats, channels), f32),
            pltpu.VMEM((tok_count + extra, channels), bf16),
            pltpu.VMEM((heads * lats, channels), bf16),
            pltpu.VMEM((heads * lats, channels), bf16),
            pltpu.VMEM((heads, lats, LANES), f32),
            pltpu.VMEM((2, heads * lats // 2, LANES), bf16),
            pltpu.VMEM((n, few, LANES), bf16),
            pltpu.VMEM((chips, few, LANES), bf16),
            pltpu.VMEM((2, chips, lats // 2, 2 * width), bf16),
            pltpu.VMEM((2, width, heads * LANES), bf16),
            pltpu.VMEM((high + 2, across // 2 + 1, 2, frames, channels), bf16),
            pltpu.VMEM((high * across // 2, 2, frames, channels), f32),
            pltpu.SemaphoreType.DMA((7,)),
            pltpu.SemaphoreType.DMA((2,)),
            pltpu.SemaphoreType.DMA((5,)),
            pltpu.SemaphoreType.DMA((units, line)),
            pltpu.SemaphoreType.DMA((units + 1,)),
            pltpu.SemaphoreType.DMA((units,)),
            pltpu.SemaphoreType.DMA((units,)),
            pltpu.SemaphoreType.DMA((units,)),
            pltpu.SemaphoreType.DMA((5,)),
            pltpu.SemaphoreType.DMA((5,)),
            pltpu.SemaphoreType.DMA((5,)),
            pltpu.SemaphoreType.DMA((5,)),
            pltpu.SemaphoreType.DMA((1,)),
            pltpu.SemaphoreType.DMA((1,)),
        ],
        compiler_params=pltpu.CompilerParams(
            collective_id=0, has_side_effects=True, vmem_limit_bytes=56 * 1024 * 1024
        ),
    )(
        maps, filters, picture_token_layer_scaling.reshape(-1, LANES), summary_probes,
        summary_probe_layer_scaling.reshape(-1, LANES), sharpness_coefficient,
        asking_projection_tensor, lookup, content, final_projection_tensor.T,
    ).astype(f32)
    return attended, (summary_probes.astype(f32) + attended).astype(bf16)


def solution(mesh):
    placed = (
        P(("groups", "wide"), None, None, None),
        P(),
        P(),
        P(),
        P(),
        P("wide", None),
        P("wide", None),
        P("wide", None),
        P(None, "wide"),
        P(),
    )
    return jax.shard_map(
        functools.partial(per_device, mesh.shape["wide"]),
        mesh=mesh,
        in_specs=placed,
        out_specs=(P("groups", None), P("groups", None)),
        check_vma=False,
    )
```

```python
import functools
import math

import jax
import jax.numpy as jnp
from jax import lax
from jax.experimental import pallas as pl
from jax.experimental.pallas import tpu as pltpu
from jax.sharding import PartitionSpec as P

RESIDUAL_SCALE = 0.2
EPSILON = 1e-06
LANES = 128
AHEAD = 3
NT = (((1,), (1,)), ((), ()))


def layer_norm(values, gain):
    center = values - jnp.mean(values, axis=-1, keepdims=True)
    spread = jnp.mean(center * center, axis=-1, keepdims=True)
    return center * lax.rsqrt(spread + EPSILON) * gain


def window(head, breadth):
    start = head * breadth // LANES * LANES
    stop = -(-(head + 1) * breadth // LANES) * LANES
    return start, stop - start


def head_mask(head, breadth, shape):
    start, width = window(head, breadth)
    lane = lax.broadcasted_iota(jnp.int32, shape, len(shape) - 1) + start
    return (lane >= head * breadth) & (lane < (head + 1) * breadth)


def halves(values):
    high = values.astype(jnp.bfloat16)
    low = (values - high.astype(jnp.float32)).astype(jnp.bfloat16)
    return high, low


def mixer(
    n, heads, chunks, blocks,
    maps_hbm, filter_hbm, gain_hbm, probes_hbm, lat_gain_hbm, sharp_ref,
    wq_hbm, wk_hbm, wv_hbm, wo_hbm,
    attended_ref,
    maps_ref, filter_ref, gain_ref, probes_ref, lat_gain_ref, wq_ref, wo_ref,
    row_of, latents, wq_wide, gathered, qpart, qcore, qrecv, qall, queries, source, u_high, u_low,
    tail, part, received, att_all, cols_all, wo_wide,
    act, summed,
    load, own_load, sent, z_recv, y_recv, x_recv, pair_recv, d_recv,
    swap_send, swap_recv, hop_send, hop_recv, head_send, head_recv,
):
    channels = latents.shape[1]
    breadth = channels // heads
    lats = probes_ref.shape[0]
    rows = lats // n
    shard = wk_hbm.shape[0]
    line = n // 4
    chips = n // 2
    cut = channels // chunks
    units = 2 * chunks
    low_lats = lats // 2
    few = heads * low_lats // chips
    me = lax.axis_index("wide")
    core = lax.rem(me, 2)
    side = lax.rem(me // 2, 2)
    at = me // 4
    chip = me // 2
    team = lax.axis_index("groups")
    odd = lax.rem(team, 2)
    third = shard // 3
    piece = pl.ds(pl.multiple_of(odd * third, third), 2 * third)
    spare = pl.ds(pl.multiple_of(odd * 2 * third, third), third)
    lacking = pl.ds(pl.multiple_of((1 - odd) * 2 * third, third), third)
    weights = (wk_hbm, wv_hbm)
    assert line >= 4
    far = True

    def place(a, b, c):
        return a * 4 + b * 2 + c

    def remote(src, dst, send, recv, target):
        return pltpu.make_async_remote_copy(
            src_ref=src, dst_ref=dst, send_sem=send, recv_sem=recv,
            device_id={"wide": target}, device_id_type=pl.DeviceIdType.MESH,
        )

    def beside(slab, send, recv):
        return pltpu.make_async_remote_copy(
            src_ref=slab, dst_ref=slab, send_sem=send, recv_sem=recv,
            device_id={"groups": team + 1 - 2 * odd, "wide": me},
            device_id_type=pl.DeviceIdType.MESH,
        )

    def each(first, count, body):
        def step(k, carry):
            body(k)
            return carry
        lax.fori_loop(first, count, step, 0)

    def columns(t):
        return t // chunks, pl.ds(pl.multiple_of(lax.rem(t, chunks) * cut, LANES), cut)

    def slab(t, b, a, rows_of):
        w, cols = columns(t)
        return gathered.at[w, core, b, a, rows_of, cols]

    def slabs(t, b, count, rows_of):
        w, cols = columns(t)
        return gathered.at[w, core, b, :count, rows_of, cols]

    def along(t, a):
        own = slab(t, side, at, piece)
        return remote(own, own, sent.at[0], z_recv.at[t, at], place(a, side, core))

    def along_far(t, a):
        block = slab(t, side, a, piece)
        return remote(
            block, block, sent.at[0], z_recv.at[t, a],
            place(jnp.where(a == 0, line - 1, 0), side, core))

    def over_side(block, recv):
        return remote(block, block, sent.at[1], recv, place(at, 1 - side, core))

    def across_own(b):
        return over_side(gathered.at[:, core, b, at, piece], y_recv.at[units])

    def across(t, a):
        return over_side(slab(t, side, a, piece), y_recv.at[t])

    def aside(t, a):
        return beside(slab(t, side, a, spare), sent.at[2], x_recv.at[t])

    def aside_all(t, rows_of):
        return beside(slabs(t, 1 - side, line, rows_of), sent.at[3], pair_recv.at[t])

    def over(t, c):
        w, cols = columns(t)
        block = gathered.at[w, c, :, :, :, cols]
        return remote(
            block, block, sent.at[4], d_recv.at[t], place(at, side, 1 - core))

    def direct(a):
        if not far:
            return a != at
        return (a != at) & (jnp.abs(a - at) != line - 1)

    def relays(a):
        if not far:
            return None
        return ((at == line - 2) & (a == 0)) | ((at == 1) & (a == line - 1))

    def nearest(k):
        low = at < (line + 1) // 2
        seen = jnp.where(low, at, line - 1 - at)
        a = jnp.where(k - 1 < seen, k - 1, k)
        return jnp.where(low, a, line - 1 - a)

    def send_own(t):
        def one(k):
            a = nearest(k)

            @pl.when(direct(a))
            def _():
                along(t, a).start()
        each(1, line, one)

    def from_line(t):
        def one(k):
            a = nearest(k)
            own = slab(t, side, a, piece)
            remote(own, own, sent.at[0], z_recv.at[t, a], place(a, side, core)).wait_recv()
            if far:
                @pl.when(relays(a))
                def _():
                    along_far(t, a).start()
            across(t, a).start()
            aside(t, a).start()
        each(1, line, one)

    def from_across(t):
        if isinstance(t, int) and t == 0:
            across_own(1 - side).wait_recv()
        over_side(slabs(t, 1 - side, line - 1, piece), y_recv.at[t]).wait_recv()
        aside_all(t, spare).start()

    def from_beside(t):
        beside(slabs(t, side, line - 1, lacking), sent.at[2], x_recv.at[t]).wait_recv()
        aside_all(t, lacking).wait_recv()
        over(t, core).start()

    def advance_line(t):
        if t < units:
            from_line(t)
        if t + AHEAD < units:
            send_own(t + AHEAD)

    def advance_rest(t):
        if 1 <= t <= units:
            from_across(t - 1)
        if 2 <= t <= units + 1:
            from_beside(t - 2)
        if 3 <= t <= units + 2:
            over(t - 3, 1 - core).wait_recv()

    def advance(t):
        advance_line(t)
        advance_rest(t)

    def finish_sends():
        def done(k, block):
            remote(block, block, sent.at[k], z_recv.at[0, 0], place(at, side, 1 - core)).wait_send()

        done(0, gathered.at[:, core, side, :line - 2, piece])
        end = (at == 0) | (at == line - 1)
        pl.when(jnp.logical_not(end))(lambda: done(0, gathered.at[:, core, side, 0, piece]))
        pl.when((at == 1) | (at == line - 2))(
            lambda: done(0, gathered.at[:, core, side, 0, piece]))
        done(1, gathered.at[:, core, side, :, piece])
        done(2, gathered.at[:, core, side, :line - 1, spare])
        done(3, gathered.at[:, core, side, :, spare])
        done(4, gathered.at[:, core])

    def peer(k):
        return lax.rem(chip + k, chips)

    def share(slot, src, dst, target):
        return remote(
            src, dst, swap_send.at[slot], swap_recv.at[slot], target * 2 + core)

    def share_start(slot, src_of, dst):
        each(1, chips, lambda k: share(slot, src_of(peer(k)), dst, peer(k)).start())

    def share_wait(slot, most):
        share(slot, most, most, peer(1)).wait_send()
        share(slot, most, most, peer(1)).wait_recv()

    def hop(slot, src, dst):
        return remote(
            src, dst, hop_send.at[slot], hop_recv.at[slot], place(at, side, 1 - core))

    def spread_start(slot, everyone):
        mine = everyone.at[core, chip]
        share_start(slot, lambda k: mine, mine)

    def spread_hop(slot, everyone):
        share_wait(slot, everyone.at[core, :chips - 1])
        hop(slot, everyone.at[core], everyone.at[core]).start()

    def spread_wait(slot, everyone):
        hop(slot, everyone.at[core], everyone.at[core]).wait_send()
        hop(slot, everyone.at[1 - core], everyone.at[1 - core]).wait_recv()

    taken = [
        pltpu.make_async_copy(src, dst, load.at[k])
        for k, (src, dst) in enumerate((
            (probes_hbm, probes_ref), (lat_gain_hbm, lat_gain_ref), (wq_hbm, wq_ref),
            (maps_hbm, maps_ref), (gain_hbm, gain_ref), (filter_hbm, filter_ref),
            (wo_hbm, wo_ref.at[core]),
        ))
    ]
    owned = [
        pltpu.make_async_copy(weights[w], gathered.at[w, core, side, at], own_load.at[w])
        for w in range(2)
    ]
    barrier = pltpu.get_barrier_semaphore()
    each(1, n, lambda k: pl.semaphore_signal(
        barrier, inc=1, device_id={"wide": lax.rem(me + k, n)},
        device_id_type=pl.DeviceIdType.MESH))
    pl.semaphore_signal(
        barrier, inc=1, device_id={"groups": team + 1 - 2 * odd, "wide": me},
        device_id_type=pl.DeviceIdType.MESH)
    for copy in owned + taken:
        copy.start()
    for copy in owned:
        copy.wait()
    pl.semaphore_wait(barrier, n)
    send_own(0)
    across_own(side).start()
    lanes_all = lax.broadcasted_iota(jnp.int32, (1, channels), 1)
    sharp = jnp.zeros((1, channels), jnp.float32)
    for head in range(heads):
        inside = (lanes_all >= head * breadth) & (lanes_all < (head + 1) * breadth)
        sharp = jnp.where(inside, sharp_ref[head], sharp)
    row_of[2:3] = sharp / math.sqrt(breadth)
    wq_wide[...] = jnp.zeros_like(wq_wide)
    for copy in taken[:3]:
        copy.wait()
    for k in range(channels // LANES):
        row_of[1:2, k * LANES:(k + 1) * LANES] = lat_gain_ref[k:k + 1]
    latents[...] = layer_norm(
        probes_ref[...].astype(jnp.float32), row_of[1:2]).astype(jnp.bfloat16).astype(jnp.float32)
    deep = wq_wide.shape[0]
    begin = pl.multiple_of(
        jnp.minimum(me * shard // LANES * LANES, channels - deep), LANES)
    wq_wide[pl.ds(pl.multiple_of(me * shard - begin, 8), shard)] = wq_ref[...].astype(jnp.float32)
    partial = jnp.dot(
        latents[:, pl.ds(begin, deep)].astype(jnp.bfloat16), wq_wide[...].astype(jnp.bfloat16),
        preferred_element_type=jnp.float32)
    for j in range(n):
        qpart[j // chips, j % chips] = partial[j * rows:(j + 1) * rows]
    hop(3, qpart.at[1 - core], qcore).start()

    def q_pair():
        hop(3, qpart.at[1 - core], qcore).wait()
        qpart[core] += qcore[...]
        qrecv[chip] = qpart[core, chip]
        share_start(0, lambda k: qpart.at[core, k], qrecv.at[chip])

    def q_sum():
        share_wait(0, qrecv.at[:chips - 1])
        qall[core, chip] = jnp.sum(qrecv[...], axis=0) * row_of[2:3]
        spread_start(1, qall)

    def q_hop():
        spread_hop(1, qall)

    def q_done():
        spread_wait(1, qall)
        for j in range(n):
            queries[j * rows:(j + 1) * rows] = qall[j // chips, j % chips]

    pairs = maps_ref.shape[0]
    frames = maps_ref.shape[2]
    high = act.shape[0] - 2
    half = act.shape[1] - 1
    group = filter_ref.shape[0] // 9
    tok_count = pairs * 2 * frames
    first_own = me * rows // 8 * 8

    act[0] = jnp.zeros(act.shape[1:], jnp.bfloat16)
    act[high + 1] = jnp.zeros(act.shape[1:], jnp.bfloat16)
    act[:, 0, 0] = jnp.zeros((high + 2, frames, channels), jnp.bfloat16)
    act[:, half, 1] = jnp.zeros((high + 2, frames, channels), jnp.bfloat16)
    own_rows = latents[pl.ds(pl.multiple_of(first_own, 8), 8)]
    source[tok_count:] = jnp.concatenate(
        [own_rows, jnp.zeros_like(own_rows)], axis=0).astype(jnp.bfloat16)
    q_pair()
    for t in range(1, AHEAD):
        send_own(t)
    taken[3].wait()

    def activate(i):
        g = jax.nn.gelu(maps_ref[i].astype(jnp.float32)).astype(jnp.bfloat16)
        y, p = i // half, lax.rem(i, half)
        act[y + 1, p, 1] = g[0]
        act[y + 1, p + 1, 0] = g[1]

    each(0, pairs, activate)
    taken[4].wait()
    taken[5].wait()
    for k in range(channels // LANES):
        row_of[0:1, k * LANES:(k + 1) * LANES] = gain_ref[k:k + 1]

    def convolve(c):
        lanes = pl.ds(pl.multiple_of(c * group, LANES), group)
        taps = jnp.concatenate([
            act[dy:dy + high, j // 2:j // 2 + half, j % 2, :, lanes].reshape(-1, group)
            for dy in range(3) for j in range(4)
        ], axis=1)
        none = jnp.zeros((group, group), jnp.bfloat16)

        def tap(dy, dx):
            if not 0 <= dx < 3:
                return none
            return filter_ref[(dy * 3 + dx) * group:(dy * 3 + dx + 1) * group, lanes]

        kernel = jnp.concatenate([
            jnp.concatenate([tap(dy, j), tap(dy, j - 1)], axis=1)
            for dy in range(3) for j in range(4)
        ], axis=0)
        both = jnp.dot(taps, kernel, preferred_element_type=jnp.float32)
        both = both.reshape(pairs, frames, 2 * group)
        summed[:, 0, :, lanes] = both[:, :, :group]
        summed[:, 1, :, lanes] = both[:, :, group:]

    def normalize(i):
        value = maps_ref[i].astype(jnp.float32) + RESIDUAL_SCALE * summed[i]
        value = layer_norm(value.reshape(2 * frames, channels), row_of[0:1])
        where = pl.multiple_of(i * 2 * frames, 16)
        source[pl.ds(where, 2 * frames)] = value.astype(jnp.bfloat16)

    parts = channels // group
    together = 5 if pairs % 5 == 0 else 1

    def normalize_some(i):
        for k in range(together):
            normalize(i * together + k)

    advance(0)
    each(0, parts // 2, convolve)
    taken[6].wait()
    hop(2, wo_ref.at[core], wo_ref.at[core]).start()
    advance(1)
    q_sum()
    each(parts // 2, parts, convolve)
    advance(2)
    each(0, pairs // together // 2, normalize_some)
    advance(3)
    each(pairs // together // 2, pairs // together, normalize_some)
    spread_wait(2, wo_ref)
    wo_wide[...] = jnp.zeros_like(wo_wide)
    for c in range(2):
        for head in range(heads):
            wo_wide[c, :, head * LANES:head * LANES + breadth] = (
                wo_ref[c, :, head * breadth:(head + 1) * breadth])
    q_hop()
    advance(4)
    q_done()

    per_block = heads // blocks
    lane = lax.broadcasted_iota(jnp.int32, (lats, LANES), 1)

    def weight(w, window_of):
        return jnp.concatenate(
            [gathered[w, j % 2, j // 2 % 2, j // 4, :, window_of] for j in range(n)], axis=0
        ).astype(jnp.bfloat16)

    def attend(first, between):
        block = slice(first * breadth, (first + per_block) * breadth)
        some = queries[:, block]
        at_lane = lax.broadcasted_iota(jnp.int32, some.shape, 1)
        asked = jnp.concatenate([
            jnp.where((at_lane >= i * breadth) & (at_lane < (i + 1) * breadth), some, 0.0)
            for i in range(per_block)
        ], axis=0)
        look = weight(0, block)
        raw = lax.dot_general(
            jnp.concatenate(halves(asked), axis=0), look, NT, preferred_element_type=jnp.float32)
        high, low = halves(raw[:per_block * lats] + raw[per_block * lats:])
        scores = lax.dot_general(high, source[...], NT, preferred_element_type=jnp.float32)
        scores += lax.dot_general(low, source[...], NT, preferred_element_type=jnp.float32)
        between()
        column = lax.broadcasted_iota(jnp.int32, scores.shape, 1)
        own = column - tok_count - (me * rows - first_own)
        live = (column < tok_count) | ((own >= 0) & (own < rows))
        scores = jnp.where(live, scores, -jnp.inf)
        row_max = jnp.max(scores, axis=1, keepdims=True)
        terms = jnp.exp(scores - row_max).astype(jnp.bfloat16)
        row_sum = jnp.sum(terms.astype(jnp.float32), axis=1, keepdims=True)
        mixed = jnp.dot(terms, source[...], preferred_element_type=jnp.float32)
        high, low = halves(mixed)
        u_high[first * lats:(first + per_block) * lats] = high
        u_low[first * lats:(first + per_block) * lats] = low
        for i in range(per_block):
            kept = jnp.zeros((lats, LANES), jnp.float32)
            spot = breadth
            for value in (row_max, row_sum):
                rest = value[i * lats:(i + 1) * lats]
                for _ in range(3):
                    top = rest.astype(jnp.bfloat16).astype(jnp.float32)
                    kept = jnp.where(lane == spot, top, kept)
                    rest = rest - top
                    spot += 1
            tail[first + i] = kept

    def project(first):
        for head in range(first, first + per_block):
            start, width = window(head, breadth)
            both = jnp.concatenate(
                [u_high[head * lats:(head + 1) * lats], u_low[head * lats:(head + 1) * lats]],
                axis=0)
            content = weight(1, slice(start, start + width))
            raw = jnp.dot(both, content, preferred_element_type=jnp.float32)
            raw = raw[:lats] + raw[lats:]
            shift = head * breadth - start
            if shift:
                raw = pltpu.roll(raw, width - shift, 1)
            raw = jnp.where(lane < breadth, raw[:, :LANES], tail[head])
            raw = raw.astype(jnp.bfloat16)
            for c in range(2):
                part[c, head * low_lats:(head + 1) * low_lats] = (
                    raw[c * low_lats:(c + 1) * low_lats])
            for k in range(head * low_lats // few, (head + 1) * low_lats // few):
                for c in range(2):
                    to_owner(k, c)

    def to_owner(k, c):
        own = part.at[c, k * few:(k + 1) * few]

        @pl.when(me != k * 2 + c)
        def _():
            remote(own, received.at[me], head_send.at[0], head_recv.at[0], k * 2 + c).start()

        @pl.when(me == k * 2 + c)
        def _():
            received[me] = part[c, k * few:(k + 1) * few]

    def ready(q, w):
        return w * chunks + -(-(q + 1) * per_block * breadth // cut) + 2

    step = 5
    for w in range(2):
        for q in range(blocks):
            while step <= ready(q, w):
                advance(step)
                step += 1
            if w == 0:
                attend(q * per_block, lambda: advance_line(step))
                advance_rest(step)
                step += 1
            else:
                project(q * per_block)

    most = received.at[:n - 1]
    remote(most, most, head_send.at[0], head_recv.at[0], lax.rem(me + 1, n)).wait_recv()
    got = received[...].astype(jnp.float32)

    def number(spot):
        return got[:, :, spot:spot + 1] + got[:, :, spot + 1:spot + 2] + got[:, :, spot + 2:spot + 3]

    maxima = number(breadth)
    factor = jnp.exp(maxima - jnp.max(maxima, axis=0, keepdims=True))
    joint = jnp.sum(number(breadth + 3) * factor, axis=0)
    whole = jnp.sum(got * factor, axis=0) / joint
    narrow = lax.broadcasted_iota(jnp.int32, whole.shape, 1) < breadth
    att_all[chip] = jnp.where(narrow, whole, 0.0).astype(jnp.bfloat16)
    mine = att_all.at[chip]
    share_start(2, lambda k: mine, mine)
    share_wait(2, att_all.at[:chips - 1])
    pieces = low_lats // few if few < low_lats else 1
    heads_at = few // low_lats if few > low_lats else 1
    joined = []
    for head in range(heads):
        if few >= low_lats:
            first = head % heads_at * low_lats
            joined.append(att_all[head // heads_at, first:first + low_lats])
        else:
            joined.append(jnp.concatenate(
                [att_all[head * pieces + i] for i in range(pieces)], axis=0))
    joined = jnp.concatenate(joined, axis=1)
    wide = wo_ref.shape[1]
    for c in range(2):
        cols = lax.dot_general(joined, wo_wide[c], NT, preferred_element_type=jnp.float32)
        cols_all[core, chip, :, c * wide:(c + 1) * wide] = cols.astype(jnp.bfloat16)
    spread_start(4, cols_all)
    spread_hop(4, cols_all)
    spread_wait(4, cols_all)
    for c in range(2):
        for k in range(chips):
            attended_ref[c * low_lats:(c + 1) * low_lats, k * 2 * wide:(k + 1) * 2 * wide] = (
                cols_all[c, k])
    remote(most, most, head_send.at[0], head_recv.at[0], lax.rem(me + 1, n)).wait_send()
    finish_sends()


def per_device(
    n,
    picture_feature_maps,
    partitioned_filter_tensor,
    picture_token_layer_scaling,
    summary_probes,
    summary_probe_layer_scaling,
    asking_projection_tensor,
    lookup_projection_tensor,
    content_projection_tensor,
    final_projection_tensor,
    sharpness_coefficient,
):
    frames, high, across, channels = picture_feature_maps.shape
    heads = sharpness_coefficient.shape[0]
    lats = summary_probes.shape[0]
    maps = picture_feature_maps.transpose(1, 2, 0, 3)
    maps = maps.reshape(high * across // 2, 2, frames, channels)
    filters = partitioned_filter_tensor.reshape(-1, channels)
    tok_count = frames * high * across
    shard = asking_projection_tensor.shape[0]
    rows = lats // n
    extra = 16
    lookup, content = lookup_projection_tensor, content_projection_tensor
    wire = jnp.bfloat16 if shard % 16 == 0 else jnp.float32
    lookup, content = lookup.astype(wire), content.astype(wire)
    anywhere = pl.BlockSpec(memory_space=pl.ANY)
    vmem = pl.BlockSpec(memory_space=pltpu.VMEM)
    smem = pl.BlockSpec(memory_space=pltpu.SMEM)
    f32, bf16 = jnp.float32, jnp.bfloat16
    width = final_projection_tensor.shape[1]
    line = n // 4
    chips = n // 2
    chunks, blocks = 4, 4
    units = 2 * chunks
    few = lats * heads // n
    attended = pl.pallas_call(
        functools.partial(mixer, n, heads, chunks, blocks),
        out_shape=jax.ShapeDtypeStruct((lats, channels), bf16),
        in_specs=[anywhere] * 5 + [smem] + [anywhere] * 4,
        out_specs=vmem,
        scratch_shapes=[
            pltpu.VMEM(maps.shape, bf16),
            pltpu.VMEM(filters.shape, bf16),
            pltpu.VMEM((channels // LANES, LANES), f32),
            pltpu.VMEM((lats, channels), bf16),
            pltpu.VMEM((channels // LANES, LANES), f32),
            pltpu.VMEM((shard, channels), bf16),
            pltpu.VMEM((2, width, channels), bf16),
            pltpu.VMEM((8, channels), f32),
            pltpu.VMEM((lats, channels), f32),
            pltpu.VMEM((2 * LANES, channels), f32),
            pltpu.VMEM((2, 2, 2, line, shard, channels), wire),
            pltpu.VMEM((2, chips, rows, channels), f32),
            pltpu.VMEM((chips, rows, channels), f32),
            pltpu.VMEM((chips, rows, channels), f32),
            pltpu.VMEM((2, chips, rows, channels), f32),
            pltpu.VMEM((lats, channels), f32),
            pltpu.VMEM((tok_count + extra, channels), bf16),
            pltpu.VMEM((heads * lats, channels), bf16),
            pltpu.VMEM((heads * lats, channels), bf16),
            pltpu.VMEM((heads, lats, LANES), f32),
            pltpu.VMEM((2, heads * lats // 2, LANES), bf16),
            pltpu.VMEM((n, few, LANES), bf16),
            pltpu.VMEM((chips, few, LANES), bf16),
            pltpu.VMEM((2, chips, lats // 2, 2 * width), bf16),
            pltpu.VMEM((2, width, heads * LANES), bf16),
            pltpu.VMEM((high + 2, across // 2 + 1, 2, frames, channels), bf16),
            pltpu.VMEM((high * across // 2, 2, frames, channels), f32),
            pltpu.SemaphoreType.DMA((7,)),
            pltpu.SemaphoreType.DMA((2,)),
            pltpu.SemaphoreType.DMA((5,)),
            pltpu.SemaphoreType.DMA((units, line)),
            pltpu.SemaphoreType.DMA((units + 1,)),
            pltpu.SemaphoreType.DMA((units,)),
            pltpu.SemaphoreType.DMA((units,)),
            pltpu.SemaphoreType.DMA((units,)),
            pltpu.SemaphoreType.DMA((5,)),
            pltpu.SemaphoreType.DMA((5,)),
            pltpu.SemaphoreType.DMA((5,)),
            pltpu.SemaphoreType.DMA((5,)),
            pltpu.SemaphoreType.DMA((1,)),
            pltpu.SemaphoreType.DMA((1,)),
        ],
        compiler_params=pltpu.CompilerParams(
            collective_id=0, has_side_effects=True, vmem_limit_bytes=56 * 1024 * 1024
        ),
    )(
        maps, filters, picture_token_layer_scaling.reshape(-1, LANES), summary_probes,
        summary_probe_layer_scaling.reshape(-1, LANES), sharpness_coefficient,
        asking_projection_tensor, lookup, content, final_projection_tensor.T,
    ).astype(f32)
    return attended, (summary_probes.astype(f32) + attended).astype(bf16)


def solution(mesh):
    placed = (
        P(("groups", "wide"), None, None, None),
        P(),
        P(),
        P(),
        P(),
        P("wide", None),
        P("wide", None),
        P("wide", None),
        P(None, "wide"),
        P(),
    )
    return jax.shard_map(
        functools.partial(per_device, mesh.shape["wide"]),
        mesh=mesh,
        in_specs=placed,
        out_specs=(P("groups", None), P("groups", None)),
        check_vma=False,
    )
```

```python
import functools
import math

import jax
import jax.numpy as jnp
from jax import lax
from jax.experimental import pallas as pl
from jax.experimental.pallas import tpu as pltpu
from jax.sharding import PartitionSpec as P

RESIDUAL_SCALE = 0.2
EPSILON = 1e-06
LANES = 128
AHEAD = 3
NT = (((1,), (1,)), ((), ()))


def layer_norm(values, gain):
    center = values - jnp.mean(values, axis=-1, keepdims=True)
    spread = jnp.mean(center * center, axis=-1, keepdims=True)
    return center * lax.rsqrt(spread + EPSILON) * gain


def window(head, breadth):
    start = head * breadth // LANES * LANES
    stop = -(-(head + 1) * breadth // LANES) * LANES
    return start, stop - start


def head_mask(head, breadth, shape):
    start, width = window(head, breadth)
    lane = lax.broadcasted_iota(jnp.int32, shape, len(shape) - 1) + start
    return (lane >= head * breadth) & (lane < (head + 1) * breadth)


def halves(values):
    high = values.astype(jnp.bfloat16)
    low = (values - high.astype(jnp.float32)).astype(jnp.bfloat16)
    return high, low


def mixer(
    n, heads, chunks, blocks,
    maps_hbm, filter_hbm, gain_hbm, probes_hbm, lat_gain_hbm, sharp_ref,
    wq_hbm, wk_hbm, wv_hbm, wo_hbm,
    attended_ref,
    maps_ref, filter_ref, gain_ref, probes_ref, lat_gain_ref, wq_ref, wo_ref,
    row_of, latents, wq_wide, gathered, qpart, qcore, qrecv, qall, queries, source, u_high, u_low,
    tail, part, received, att_all, cols_all, wo_wide,
    act, summed,
    load, own_load, sent, z_recv, y_recv, x_recv, pair_recv, d_recv,
    swap_send, swap_recv, hop_send, hop_recv, head_send, head_recv,
):
    channels = latents.shape[1]
    breadth = channels // heads
    lats = probes_ref.shape[0]
    rows = lats // n
    shard = wk_hbm.shape[0]
    line = n // 4
    chips = n // 2
    cut = channels // chunks
    units = 2 * chunks
    low_lats = lats // 2
    few = heads * low_lats // chips
    me = lax.axis_index("wide")
    core = lax.rem(me, 2)
    side = lax.rem(me // 2, 2)
    at = me // 4
    chip = me // 2
    team = lax.axis_index("groups")
    odd = lax.rem(team, 2)
    third = shard // 3
    piece = pl.ds(pl.multiple_of(odd * third, third), 2 * third)
    spare = pl.ds(pl.multiple_of(odd * 2 * third, third), third)
    lacking = pl.ds(pl.multiple_of((1 - odd) * 2 * third, third), third)
    weights = (wk_hbm, wv_hbm)
    assert line >= 4
    far = True

    def place(a, b, c):
        return a * 4 + b * 2 + c

    def remote(src, dst, send, recv, target):
        return pltpu.make_async_remote_copy(
            src_ref=src, dst_ref=dst, send_sem=send, recv_sem=recv,
            device_id={"wide": target}, device_id_type=pl.DeviceIdType.MESH,
        )

    def beside(slab, send, recv):
        return pltpu.make_async_remote_copy(
            src_ref=slab, dst_ref=slab, send_sem=send, recv_sem=recv,
            device_id={"groups": team + 1 - 2 * odd, "wide": me},
            device_id_type=pl.DeviceIdType.MESH,
        )

    def each(first, count, body):
        def step(k, carry):
            body(k)
            return carry
        lax.fori_loop(first, count, step, 0)

    def columns(t):
        return t // chunks, pl.ds(pl.multiple_of(lax.rem(t, chunks) * cut, LANES), cut)

    def slab(t, b, a, rows_of):
        w, cols = columns(t)
        return gathered.at[w, core, b, a, rows_of, cols]

    def slabs(t, b, count, rows_of):
        w, cols = columns(t)
        return gathered.at[w, core, b, :count, rows_of, cols]

    def along(t, a):
        own = slab(t, side, at, piece)
        return remote(own, own, sent.at[0], z_recv.at[t, at], place(a, side, core))

    def along_far(t, a):
        block = slab(t, side, a, piece)
        return remote(
            block, block, sent.at[0], z_recv.at[t, a],
            place(jnp.where(a == 0, line - 1, 0), side, core))

    def over_side(block, recv):
        return remote(block, block, sent.at[1], recv, place(at, 1 - side, core))

    def across_own(b):
        return over_side(gathered.at[:, core, b, at, piece], y_recv.at[units])

    def across(t, a):
        return over_side(slab(t, side, a, piece), y_recv.at[t])

    def aside(t, a):
        return beside(slab(t, side, a, spare), sent.at[2], x_recv.at[t])

    def aside_all(t, rows_of):
        return beside(slabs(t, 1 - side, line, rows_of), sent.at[3], pair_recv.at[t])

    def over(t, c):
        w, cols = columns(t)
        block = gathered.at[w, c, :, :, :, cols]
        return remote(
            block, block, sent.at[4], d_recv.at[t], place(at, side, 1 - core))

    def direct(a):
        if not far:
            return a != at
        return (a != at) & (jnp.abs(a - at) != line - 1)

    def relays(a):
        if not far:
            return None
        return ((at == line - 2) & (a == 0)) | ((at == 1) & (a == line - 1))

    def nearest(k):
        low = at < (line + 1) // 2
        seen = jnp.where(low, at, line - 1 - at)
        a = jnp.where(k - 1 < seen, k - 1, k)
        return jnp.where(low, a, line - 1 - a)

    def send_own(t):
        def one(k):
            a = nearest(k)

            @pl.when(direct(a))
            def _():
                along(t, a).start()
        each(1, line, one)

    def from_line(t):
        def one(k):
            a = nearest(k)
            own = slab(t, side, a, piece)
            remote(own, own, sent.at[0], z_recv.at[t, a], place(a, side, core)).wait_recv()
            if far:
                @pl.when(relays(a))
                def _():
                    along_far(t, a).start()
            across(t, a).start()
            aside(t, a).start()
        each(1, line, one)

    def from_across(t):
        if isinstance(t, int) and t == 0:
            across_own(1 - side).wait_recv()
        over_side(slabs(t, 1 - side, line - 1, piece), y_recv.at[t]).wait_recv()
        aside_all(t, spare).start()

    def from_beside(t):
        beside(slabs(t, side, line - 1, lacking), sent.at[2], x_recv.at[t]).wait_recv()
        aside_all(t, lacking).wait_recv()
        over(t, core).start()

    def advance_line(t):
        if t < units:
            from_line(t)
        if t + AHEAD < units:
            send_own(t + AHEAD)

    def advance_rest(t):
        if 1 <= t <= units:
            from_across(t - 1)
        if 2 <= t <= units + 1:
            from_beside(t - 2)
        if 3 <= t <= units + 2:
            over(t - 3, 1 - core).wait_recv()

    def advance(t):
        advance_line(t)
        advance_rest(t)

    def finish_sends():
        def done(k, block):
            remote(block, block, sent.at[k], z_recv.at[0, 0], place(at, side, 1 - core)).wait_send()

        done(0, gathered.at[:, core, side, :line - 2, piece])
        end = (at == 0) | (at == line - 1)
        pl.when(jnp.logical_not(end))(lambda: done(0, gathered.at[:, core, side, 0, piece]))
        pl.when((at == 1) | (at == line - 2))(
            lambda: done(0, gathered.at[:, core, side, 0, piece]))
        done(1, gathered.at[:, core, side, :, piece])
        done(2, gathered.at[:, core, side, :line - 1, spare])
        done(3, gathered.at[:, core, side, :, spare])
        done(4, gathered.at[:, core])

    def peer(k):
        return lax.rem(chip + k, chips)

    def share(slot, src, dst, target):
        return remote(
            src, dst, swap_send.at[slot], swap_recv.at[slot], target * 2 + core)

    def share_start(slot, src_of, dst):
        each(1, chips, lambda k: share(slot, src_of(peer(k)), dst, peer(k)).start())

    def share_wait(slot, most):
        share(slot, most, most, peer(1)).wait_send()
        share(slot, most, most, peer(1)).wait_recv()

    def hop(slot, src, dst):
        return remote(
            src, dst, hop_send.at[slot], hop_recv.at[slot], place(at, side, 1 - core))

    def spread_start(slot, everyone):
        mine = everyone.at[core, chip]
        share_start(slot, lambda k: mine, mine)

    def spread_hop(slot, everyone):
        share_wait(slot, everyone.at[core, :chips - 1])
        hop(slot, everyone.at[core], everyone.at[core]).start()

    def spread_wait(slot, everyone):
        hop(slot, everyone.at[core], everyone.at[core]).wait_send()
        hop(slot, everyone.at[1 - core], everyone.at[1 - core]).wait_recv()

    taken = [
        pltpu.make_async_copy(src, dst, load.at[k])
        for k, (src, dst) in enumerate((
            (probes_hbm, probes_ref), (lat_gain_hbm, lat_gain_ref), (wq_hbm, wq_ref),
            (maps_hbm, maps_ref), (gain_hbm, gain_ref), (filter_hbm, filter_ref),
            (wo_hbm, wo_ref.at[core]),
        ))
    ]
    owned = [
        pltpu.make_async_copy(weights[w], gathered.at[w, core, side, at], own_load.at[w])
        for w in range(2)
    ]
    barrier = pltpu.get_barrier_semaphore()
    each(1, n, lambda k: pl.semaphore_signal(
        barrier, inc=1, device_id={"wide": lax.rem(me + k, n)},
        device_id_type=pl.DeviceIdType.MESH))
    pl.semaphore_signal(
        barrier, inc=1, device_id={"groups": team + 1 - 2 * odd, "wide": me},
        device_id_type=pl.DeviceIdType.MESH)
    for copy in owned + taken:
        copy.start()
    for copy in owned:
        copy.wait()
    pl.semaphore_wait(barrier, n)
    send_own(0)
    across_own(side).start()
    lanes_all = lax.broadcasted_iota(jnp.int32, (1, channels), 1)
    sharp = jnp.zeros((1, channels), jnp.float32)
    for head in range(heads):
        inside = (lanes_all >= head * breadth) & (lanes_all < (head + 1) * breadth)
        sharp = jnp.where(inside, sharp_ref[head], sharp)
    row_of[2:3] = sharp / math.sqrt(breadth)
    wq_wide[...] = jnp.zeros_like(wq_wide)
    for copy in taken[:3]:
        copy.wait()
    for k in range(channels // LANES):
        row_of[1:2, k * LANES:(k + 1) * LANES] = lat_gain_ref[k:k + 1]
    latents[...] = layer_norm(
        probes_ref[...].astype(jnp.float32), row_of[1:2]).astype(jnp.bfloat16).astype(jnp.float32)
    deep = wq_wide.shape[0]
    begin = pl.multiple_of(
        jnp.minimum(me * shard // LANES * LANES, channels - deep), LANES)
    wq_wide[pl.ds(pl.multiple_of(me * shard - begin, 8), shard)] = wq_ref[...].astype(jnp.float32)
    partial = jnp.dot(
        latents[:, pl.ds(begin, deep)].astype(jnp.bfloat16), wq_wide[...].astype(jnp.bfloat16),
        preferred_element_type=jnp.float32)
    for j in range(n):
        qpart[j // chips, j % chips] = partial[j * rows:(j + 1) * rows]
    hop(3, qpart.at[1 - core], qcore).start()

    def q_pair():
        hop(3, qpart.at[1 - core], qcore).wait()
        qpart[core] += qcore[...]
        qrecv[chip] = qpart[core, chip]
        share_start(0, lambda k: qpart.at[core, k], qrecv.at[chip])

    def q_sum():
        share_wait(0, qrecv.at[:chips - 1])
        qall[core, chip] = jnp.sum(qrecv[...], axis=0) * row_of[2:3]
        spread_start(1, qall)

    def q_hop():
        spread_hop(1, qall)

    def q_done():
        spread_wait(1, qall)
        for j in range(n):
            queries[j * rows:(j + 1) * rows] = qall[j // chips, j % chips]

    pairs = maps_ref.shape[0]
    frames = maps_ref.shape[2]
    high = act.shape[0] - 2
    half = act.shape[1] - 1
    group = filter_ref.shape[0] // 9
    tok_count = pairs * 2 * frames
    first_own = me * rows // 8 * 8

    act[0] = jnp.zeros(act.shape[1:], jnp.bfloat16)
    act[high + 1] = jnp.zeros(act.shape[1:], jnp.bfloat16)
    act[:, 0, 0] = jnp.zeros((high + 2, frames, channels), jnp.bfloat16)
    act[:, half, 1] = jnp.zeros((high + 2, frames, channels), jnp.bfloat16)
    own_rows = latents[pl.ds(pl.multiple_of(first_own, 8), 8)]
    source[tok_count:] = jnp.concatenate(
        [own_rows, jnp.zeros_like(own_rows)], axis=0).astype(jnp.bfloat16)
    q_pair()
    for t in range(1, AHEAD):
        send_own(t)
    taken[3].wait()

    def activate(i):
        g = jax.nn.gelu(maps_ref[i].astype(jnp.float32)).astype(jnp.bfloat16)
        y, p = i // half, lax.rem(i, half)
        act[y + 1, p, 1] = g[0]
        act[y + 1, p + 1, 0] = g[1]

    each(0, pairs, activate)
    taken[4].wait()
    taken[5].wait()
    for k in range(channels // LANES):
        row_of[0:1, k * LANES:(k + 1) * LANES] = gain_ref[k:k + 1]

    def convolve(c):
        lanes = pl.ds(pl.multiple_of(c * group, LANES), group)
        taps = jnp.concatenate([
            act[dy:dy + high, j // 2:j // 2 + half, j % 2, :, lanes].reshape(-1, group)
            for dy in range(3) for j in range(4)
        ], axis=1)
        none = jnp.zeros((group, group), jnp.bfloat16)

        def tap(dy, dx):
            if not 0 <= dx < 3:
                return none
            return filter_ref[(dy * 3 + dx) * group:(dy * 3 + dx + 1) * group, lanes]

        kernel = jnp.concatenate([
            jnp.concatenate([tap(dy, j), tap(dy, j - 1)], axis=1)
            for dy in range(3) for j in range(4)
        ], axis=0)
        both = jnp.dot(taps, kernel, preferred_element_type=jnp.float32)
        both = both.reshape(pairs, frames, 2 * group)
        summed[:, 0, :, lanes] = both[:, :, :group]
        summed[:, 1, :, lanes] = both[:, :, group:]

    def normalize(i):
        value = maps_ref[i].astype(jnp.float32) + RESIDUAL_SCALE * summed[i]
        value = layer_norm(value.reshape(2 * frames, channels), row_of[0:1])
        where = pl.multiple_of(i * 2 * frames, 16)
        source[pl.ds(where, 2 * frames)] = value.astype(jnp.bfloat16)

    parts = channels // group
    together = 5 if pairs % 5 == 0 else 1

    def normalize_some(i):
        for k in range(together):
            normalize(i * together + k)

    advance(0)
    each(0, parts // 2, convolve)
    taken[6].wait()
    hop(2, wo_ref.at[core], wo_ref.at[core]).start()
    advance(1)
    q_sum()
    each(parts // 2, parts, convolve)
    advance(2)
    each(0, pairs // together // 2, normalize_some)
    advance(3)
    each(pairs // together // 2, pairs // together, normalize_some)
    spread_wait(2, wo_ref)
    wo_wide[...] = jnp.zeros_like(wo_wide)
    for c in range(2):
        for head in range(heads):
            wo_wide[c, :, head * LANES:head * LANES + breadth] = (
                wo_ref[c, :, head * breadth:(head + 1) * breadth])
    q_hop()
    advance(4)
    q_done()

    per_block = heads // blocks
    lane = lax.broadcasted_iota(jnp.int32, (lats, LANES), 1)

    def weight(w, window_of):
        return jnp.concatenate(
            [gathered[w, j % 2, j // 2 % 2, j // 4, :, window_of] for j in range(n)], axis=0
        ).astype(jnp.bfloat16)

    def attend(first, early, between):
        block = slice(first * breadth, (first + per_block) * breadth)
        some = queries[:, block]
        at_lane = lax.broadcasted_iota(jnp.int32, some.shape, 1)
        asked = jnp.concatenate([
            jnp.where((at_lane >= i * breadth) & (at_lane < (i + 1) * breadth), some, 0.0)
            for i in range(per_block)
        ], axis=0)
        look = weight(0, block)
        raw = lax.dot_general(
            jnp.concatenate(halves(asked), axis=0), look, NT, preferred_element_type=jnp.float32)
        high, low = halves(raw[:per_block * lats] + raw[per_block * lats:])
        early()
        scores = lax.dot_general(high, source[...], NT, preferred_element_type=jnp.float32)
        scores += lax.dot_general(low, source[...], NT, preferred_element_type=jnp.float32)
        between()
        column = lax.broadcasted_iota(jnp.int32, scores.shape, 1)
        own = column - tok_count - (me * rows - first_own)
        live = (column < tok_count) | ((own >= 0) & (own < rows))
        scores = jnp.where(live, scores, -jnp.inf)
        row_max = jnp.max(scores, axis=1, keepdims=True)
        terms = jnp.exp(scores - row_max).astype(jnp.bfloat16)
        row_sum = jnp.sum(terms.astype(jnp.float32), axis=1, keepdims=True)
        mixed = jnp.dot(terms, source[...], preferred_element_type=jnp.float32)
        high, low = halves(mixed)
        u_high[first * lats:(first + per_block) * lats] = high
        u_low[first * lats:(first + per_block) * lats] = low
        for i in range(per_block):
            kept = jnp.zeros((lats, LANES), jnp.float32)
            spot = breadth
            for value in (row_max, row_sum):
                rest = value[i * lats:(i + 1) * lats]
                for _ in range(3):
                    top = rest.astype(jnp.bfloat16).astype(jnp.float32)
                    kept = jnp.where(lane == spot, top, kept)
                    rest = rest - top
                    spot += 1
            tail[first + i] = kept

    def project(first):
        for head in range(first, first + per_block):
            start, width = window(head, breadth)
            both = jnp.concatenate(
                [u_high[head * lats:(head + 1) * lats], u_low[head * lats:(head + 1) * lats]],
                axis=0)
            content = weight(1, slice(start, start + width))
            raw = jnp.dot(both, content, preferred_element_type=jnp.float32)
            raw = raw[:lats] + raw[lats:]
            shift = head * breadth - start
            if shift:
                raw = pltpu.roll(raw, width - shift, 1)
            raw = jnp.where(lane < breadth, raw[:, :LANES], tail[head])
            raw = raw.astype(jnp.bfloat16)
            for c in range(2):
                part[c, head * low_lats:(head + 1) * low_lats] = (
                    raw[c * low_lats:(c + 1) * low_lats])
            for k in range(head * low_lats // few, (head + 1) * low_lats // few):
                for c in range(2):
                    to_owner(k, c)

    def to_owner(k, c):
        own = part.at[c, k * few:(k + 1) * few]

        @pl.when(me != k * 2 + c)
        def _():
            remote(own, received.at[me], head_send.at[0], head_recv.at[0], k * 2 + c).start()

        @pl.when(me == k * 2 + c)
        def _():
            received[me] = part[c, k * few:(k + 1) * few]

    def ready(q, w):
        return w * chunks + -(-(q + 1) * per_block * breadth // cut) + 2

    step = 5
    for w in range(2):
        for q in range(blocks):
            while step <= ready(q, w):
                advance(step)
                step += 1
            if w == 0:
                attend(
                    q * per_block, lambda: advance_line(step), lambda: advance_rest(step))
                step += 1
            else:
                project(q * per_block)

    most = received.at[:n - 1]
    remote(most, most, head_send.at[0], head_recv.at[0], lax.rem(me + 1, n)).wait_recv()
    got = received[...].astype(jnp.float32)

    def number(spot):
        return got[:, :, spot:spot + 1] + got[:, :, spot + 1:spot + 2] + got[:, :, spot + 2:spot + 3]

    maxima = number(breadth)
    factor = jnp.exp(maxima - jnp.max(maxima, axis=0, keepdims=True))
    joint = jnp.sum(number(breadth + 3) * factor, axis=0)
    whole = jnp.sum(got * factor, axis=0) / joint
    narrow = lax.broadcasted_iota(jnp.int32, whole.shape, 1) < breadth
    att_all[chip] = jnp.where(narrow, whole, 0.0).astype(jnp.bfloat16)
    mine = att_all.at[chip]
    share_start(2, lambda k: mine, mine)
    share_wait(2, att_all.at[:chips - 1])
    pieces = low_lats // few if few < low_lats else 1
    heads_at = few // low_lats if few > low_lats else 1
    joined = []
    for head in range(heads):
        if few >= low_lats:
            first = head % heads_at * low_lats
            joined.append(att_all[head // heads_at, first:first + low_lats])
        else:
            joined.append(jnp.concatenate(
                [att_all[head * pieces + i] for i in range(pieces)], axis=0))
    joined = jnp.concatenate(joined, axis=1)
    wide = wo_ref.shape[1]
    for c in range(2):
        cols = lax.dot_general(joined, wo_wide[c], NT, preferred_element_type=jnp.float32)
        cols_all[core, chip, :, c * wide:(c + 1) * wide] = cols.astype(jnp.bfloat16)
    spread_start(4, cols_all)
    spread_hop(4, cols_all)
    spread_wait(4, cols_all)
    for c in range(2):
        for k in range(chips):
            attended_ref[c * low_lats:(c + 1) * low_lats, k * 2 * wide:(k + 1) * 2 * wide] = (
                cols_all[c, k])
    remote(most, most, head_send.at[0], head_recv.at[0], lax.rem(me + 1, n)).wait_send()
    finish_sends()


def per_device(
    n,
    picture_feature_maps,
    partitioned_filter_tensor,
    picture_token_layer_scaling,
    summary_probes,
    summary_probe_layer_scaling,
    asking_projection_tensor,
    lookup_projection_tensor,
    content_projection_tensor,
    final_projection_tensor,
    sharpness_coefficient,
):
    frames, high, across, channels = picture_feature_maps.shape
    heads = sharpness_coefficient.shape[0]
    lats = summary_probes.shape[0]
    maps = picture_feature_maps.transpose(1, 2, 0, 3)
    maps = maps.reshape(high * across // 2, 2, frames, channels)
    filters = partitioned_filter_tensor.reshape(-1, channels)
    tok_count = frames * high * across
    shard = asking_projection_tensor.shape[0]
    rows = lats // n
    extra = 16
    lookup, content = lookup_projection_tensor, content_projection_tensor
    wire = jnp.bfloat16 if shard % 16 == 0 else jnp.float32
    lookup, content = lookup.astype(wire), content.astype(wire)
    anywhere = pl.BlockSpec(memory_space=pl.ANY)
    vmem = pl.BlockSpec(memory_space=pltpu.VMEM)
    smem = pl.BlockSpec(memory_space=pltpu.SMEM)
    f32, bf16 = jnp.float32, jnp.bfloat16
    width = final_projection_tensor.shape[1]
    line = n // 4
    chips = n // 2
    chunks, blocks = 4, 4
    units = 2 * chunks
    few = lats * heads // n
    attended = pl.pallas_call(
        functools.partial(mixer, n, heads, chunks, blocks),
        out_shape=jax.ShapeDtypeStruct((lats, channels), bf16),
        in_specs=[anywhere] * 5 + [smem] + [anywhere] * 4,
        out_specs=vmem,
        scratch_shapes=[
            pltpu.VMEM(maps.shape, bf16),
            pltpu.VMEM(filters.shape, bf16),
            pltpu.VMEM((channels // LANES, LANES), f32),
            pltpu.VMEM((lats, channels), bf16),
            pltpu.VMEM((channels // LANES, LANES), f32),
            pltpu.VMEM((shard, channels), bf16),
            pltpu.VMEM((2, width, channels), bf16),
            pltpu.VMEM((8, channels), f32),
            pltpu.VMEM((lats, channels), f32),
            pltpu.VMEM((2 * LANES, channels), f32),
            pltpu.VMEM((2, 2, 2, line, shard, channels), wire),
            pltpu.VMEM((2, chips, rows, channels), f32),
            pltpu.VMEM((chips, rows, channels), f32),
            pltpu.VMEM((chips, rows, channels), f32),
            pltpu.VMEM((2, chips, rows, channels), f32),
            pltpu.VMEM((lats, channels), f32),
            pltpu.VMEM((tok_count + extra, channels), bf16),
            pltpu.VMEM((heads * lats, channels), bf16),
            pltpu.VMEM((heads * lats, channels), bf16),
            pltpu.VMEM((heads, lats, LANES), f32),
            pltpu.VMEM((2, heads * lats // 2, LANES), bf16),
            pltpu.VMEM((n, few, LANES), bf16),
            pltpu.VMEM((chips, few, LANES), bf16),
            pltpu.VMEM((2, chips, lats // 2, 2 * width), bf16),
            pltpu.VMEM((2, width, heads * LANES), bf16),
            pltpu.VMEM((high + 2, across // 2 + 1, 2, frames, channels), bf16),
            pltpu.VMEM((high * across // 2, 2, frames, channels), f32),
            pltpu.SemaphoreType.DMA((7,)),
            pltpu.SemaphoreType.DMA((2,)),
            pltpu.SemaphoreType.DMA((5,)),
            pltpu.SemaphoreType.DMA((units, line)),
            pltpu.SemaphoreType.DMA((units + 1,)),
            pltpu.SemaphoreType.DMA((units,)),
            pltpu.SemaphoreType.DMA((units,)),
            pltpu.SemaphoreType.DMA((units,)),
            pltpu.SemaphoreType.DMA((5,)),
            pltpu.SemaphoreType.DMA((5,)),
            pltpu.SemaphoreType.DMA((5,)),
            pltpu.SemaphoreType.DMA((5,)),
            pltpu.SemaphoreType.DMA((1,)),
            pltpu.SemaphoreType.DMA((1,)),
        ],
        compiler_params=pltpu.CompilerParams(
            collective_id=0, has_side_effects=True, vmem_limit_bytes=56 * 1024 * 1024
        ),
    )(
        maps, filters, picture_token_layer_scaling.reshape(-1, LANES), summary_probes,
        summary_probe_layer_scaling.reshape(-1, LANES), sharpness_coefficient,
        asking_projection_tensor, lookup, content, final_projection_tensor.T,
    ).astype(f32)
    return attended, (summary_probes.astype(f32) + attended).astype(bf16)


def solution(mesh):
    placed = (
        P(("groups", "wide"), None, None, None),
        P(),
        P(),
        P(),
        P(),
        P("wide", None),
        P("wide", None),
        P("wide", None),
        P(None, "wide"),
        P(),
    )
    return jax.shard_map(
        functools.partial(per_device, mesh.shape["wide"]),
        mesh=mesh,
        in_specs=placed,
        out_specs=(P("groups", None), P("groups", None)),
        check_vma=False,
    )
```

```python
import functools
import math

import jax
import jax.numpy as jnp
from jax import lax
from jax.experimental import pallas as pl
from jax.experimental.pallas import tpu as pltpu
from jax.sharding import PartitionSpec as P

RESIDUAL_SCALE = 0.2
EPSILON = 1e-06
LANES = 128
AHEAD = 4
NT = (((1,), (1,)), ((), ()))


def layer_norm(values, gain):
    center = values - jnp.mean(values, axis=-1, keepdims=True)
    spread = jnp.mean(center * center, axis=-1, keepdims=True)
    return center * lax.rsqrt(spread + EPSILON) * gain


def window(head, breadth):
    start = head * breadth // LANES * LANES
    stop = -(-(head + 1) * breadth // LANES) * LANES
    return start, stop - start


def head_mask(head, breadth, shape):
    start, width = window(head, breadth)
    lane = lax.broadcasted_iota(jnp.int32, shape, len(shape) - 1) + start
    return (lane >= head * breadth) & (lane < (head + 1) * breadth)


def halves(values):
    high = values.astype(jnp.bfloat16)
    low = (values - high.astype(jnp.float32)).astype(jnp.bfloat16)
    return high, low


def mixer(
    n, heads, chunks, blocks,
    maps_hbm, filter_hbm, gain_hbm, probes_hbm, lat_gain_hbm, sharp_ref,
    wq_hbm, wk_hbm, wv_hbm, wo_hbm,
    attended_ref,
    maps_ref, filter_ref, gain_ref, probes_ref, lat_gain_ref, wq_ref, wo_ref,
    row_of, latents, wq_wide, gathered, qpart, qcore, qrecv, qall, queries, source, u_high, u_low,
    tail, part, received, att_all, cols_all, wo_wide,
    act, summed,
    load, own_load, sent, z_recv, y_recv, x_recv, pair_recv, d_recv,
    swap_send, swap_recv, hop_send, hop_recv, head_send, head_recv,
):
    channels = latents.shape[1]
    breadth = channels // heads
    lats = probes_ref.shape[0]
    rows = lats // n
    shard = wk_hbm.shape[0]
    line = n // 4
    chips = n // 2
    cut = channels // chunks
    units = 2 * chunks
    low_lats = lats // 2
    few = heads * low_lats // chips
    me = lax.axis_index("wide")
    core = lax.rem(me, 2)
    side = lax.rem(me // 2, 2)
    at = me // 4
    chip = me // 2
    team = lax.axis_index("groups")
    odd = lax.rem(team, 2)
    third = shard // 3
    piece = pl.ds(pl.multiple_of(odd * third, third), 2 * third)
    spare = pl.ds(pl.multiple_of(odd * 2 * third, third), third)
    lacking = pl.ds(pl.multiple_of((1 - odd) * 2 * third, third), third)
    weights = (wk_hbm, wv_hbm)
    assert line >= 4
    far = True

    def place(a, b, c):
        return a * 4 + b * 2 + c

    def remote(src, dst, send, recv, target):
        return pltpu.make_async_remote_copy(
            src_ref=src, dst_ref=dst, send_sem=send, recv_sem=recv,
            device_id={"wide": target}, device_id_type=pl.DeviceIdType.MESH,
        )

    def beside(slab, send, recv):
        return pltpu.make_async_remote_copy(
            src_ref=slab, dst_ref=slab, send_sem=send, recv_sem=recv,
            device_id={"groups": team + 1 - 2 * odd, "wide": me},
            device_id_type=pl.DeviceIdType.MESH,
        )

    def each(first, count, body):
        def step(k, carry):
            body(k)
            return carry
        lax.fori_loop(first, count, step, 0)

    def columns(t):
        return t // chunks, pl.ds(pl.multiple_of(lax.rem(t, chunks) * cut, LANES), cut)

    def slab(t, b, a, rows_of):
        w, cols = columns(t)
        return gathered.at[w, core, b, a, rows_of, cols]

    def slabs(t, b, count, rows_of):
        w, cols = columns(t)
        return gathered.at[w, core, b, :count, rows_of, cols]

    def along(t, a):
        own = slab(t, side, at, piece)
        return remote(own, own, sent.at[0], z_recv.at[t, at], place(a, side, core))

    def along_far(t, a):
        block = slab(t, side, a, piece)
        return remote(
            block, block, sent.at[0], z_recv.at[t, a],
            place(jnp.where(a == 0, line - 1, 0), side, core))

    def over_side(block, recv):
        return remote(block, block, sent.at[1], recv, place(at, 1 - side, core))

    def across_own(b):
        return over_side(gathered.at[:, core, b, at, piece], y_recv.at[units])

    def across(t, a):
        return over_side(slab(t, side, a, piece), y_recv.at[t])

    def aside(t, a):
        return beside(slab(t, side, a, spare), sent.at[2], x_recv.at[t])

    def aside_all(t, rows_of):
        return beside(slabs(t, 1 - side, line, rows_of), sent.at[3], pair_recv.at[t])

    def over(t, c):
        w, cols = columns(t)
        block = gathered.at[w, c, :, :, :, cols]
        return remote(
            block, block, sent.at[4], d_recv.at[t], place(at, side, 1 - core))

    def direct(a):
        if not far:
            return a != at
        return (a != at) & (jnp.abs(a - at) != line - 1)

    def relays(a):
        if not far:
            return None
        return ((at == line - 2) & (a == 0)) | ((at == 1) & (a == line - 1))

    def nearest(k):
        low = at < (line + 1) // 2
        seen = jnp.where(low, at, line - 1 - at)
        a = jnp.where(k - 1 < seen, k - 1, k)
        return jnp.where(low, a, line - 1 - a)

    def send_own(t):
        def one(k):
            a = nearest(k)

            @pl.when(direct(a))
            def _():
                along(t, a).start()
        each(1, line, one)

    def from_line(t):
        def one(k):
            a = nearest(k)
            own = slab(t, side, a, piece)
            remote(own, own, sent.at[0], z_recv.at[t, a], place(a, side, core)).wait_recv()
            if far:
                @pl.when(relays(a))
                def _():
                    along_far(t, a).start()
            across(t, a).start()
            aside(t, a).start()
        each(1, line, one)

    def from_across(t):
        if isinstance(t, int) and t == 0:
            across_own(1 - side).wait_recv()
        over_side(slabs(t, 1 - side, line - 1, piece), y_recv.at[t]).wait_recv()
        aside_all(t, spare).start()

    def from_beside(t):
        beside(slabs(t, side, line - 1, lacking), sent.at[2], x_recv.at[t]).wait_recv()
        aside_all(t, lacking).wait_recv()
        over(t, core).start()

    def advance_line(t):
        if t < units:
            from_line(t)
        if t + AHEAD < units:
            send_own(t + AHEAD)

    def advance_rest(t):
        if 1 <= t <= units:
            from_across(t - 1)
        if 2 <= t <= units + 1:
            from_beside(t - 2)
        if 3 <= t <= units + 2:
            over(t - 3, 1 - core).wait_recv()

    def advance(t):
        advance_line(t)
        advance_rest(t)

    def finish_sends():
        def done(k, block):
            remote(block, block, sent.at[k], z_recv.at[0, 0], place(at, side, 1 - core)).wait_send()

        done(0, gathered.at[:, core, side, :line - 2, piece])
        end = (at == 0) | (at == line - 1)
        pl.when(jnp.logical_not(end))(lambda: done(0, gathered.at[:, core, side, 0, piece]))
        pl.when((at == 1) | (at == line - 2))(
            lambda: done(0, gathered.at[:, core, side, 0, piece]))
        done(1, gathered.at[:, core, side, :, piece])
        done(2, gathered.at[:, core, side, :line - 1, spare])
        done(3, gathered.at[:, core, side, :, spare])
        done(4, gathered.at[:, core])

    def peer(k):
        return lax.rem(chip + k, chips)

    def share(slot, src, dst, target):
        return remote(
            src, dst, swap_send.at[slot], swap_recv.at[slot], target * 2 + core)

    def share_start(slot, src_of, dst):
        each(1, chips, lambda k: share(slot, src_of(peer(k)), dst, peer(k)).start())

    def share_wait(slot, most):
        share(slot, most, most, peer(1)).wait_send()
        share(slot, most, most, peer(1)).wait_recv()

    def hop(slot, src, dst):
        return remote(
            src, dst, hop_send.at[slot], hop_recv.at[slot], place(at, side, 1 - core))

    def spread_start(slot, everyone):
        mine = everyone.at[core, chip]
        share_start(slot, lambda k: mine, mine)

    def spread_hop(slot, everyone):
        share_wait(slot, everyone.at[core, :chips - 1])
        hop(slot, everyone.at[core], everyone.at[core]).start()

    def spread_wait(slot, everyone):
        hop(slot, everyone.at[core], everyone.at[core]).wait_send()
        hop(slot, everyone.at[1 - core], everyone.at[1 - core]).wait_recv()

    taken = [
        pltpu.make_async_copy(src, dst, load.at[k])
        for k, (src, dst) in enumerate((
            (probes_hbm, probes_ref), (lat_gain_hbm, lat_gain_ref), (wq_hbm, wq_ref),
            (maps_hbm, maps_ref), (gain_hbm, gain_ref), (filter_hbm, filter_ref),
            (wo_hbm, wo_ref.at[core]),
        ))
    ]
    owned = [
        pltpu.make_async_copy(weights[w], gathered.at[w, core, side, at], own_load.at[w])
        for w in range(2)
    ]
    barrier = pltpu.get_barrier_semaphore()
    each(1, n, lambda k: pl.semaphore_signal(
        barrier, inc=1, device_id={"wide": lax.rem(me + k, n)},
        device_id_type=pl.DeviceIdType.MESH))
    pl.semaphore_signal(
        barrier, inc=1, device_id={"groups": team + 1 - 2 * odd, "wide": me},
        device_id_type=pl.DeviceIdType.MESH)
    for copy in owned + taken:
        copy.start()
    for copy in owned:
        copy.wait()
    pl.semaphore_wait(barrier, n)
    send_own(0)
    across_own(side).start()
    lanes_all = lax.broadcasted_iota(jnp.int32, (1, channels), 1)
    sharp = jnp.zeros((1, channels), jnp.float32)
    for head in range(heads):
        inside = (lanes_all >= head * breadth) & (lanes_all < (head + 1) * breadth)
        sharp = jnp.where(inside, sharp_ref[head], sharp)
    row_of[2:3] = sharp / math.sqrt(breadth)
    wq_wide[...] = jnp.zeros_like(wq_wide)
    for copy in taken[:3]:
        copy.wait()
    for k in range(channels // LANES):
        row_of[1:2, k * LANES:(k + 1) * LANES] = lat_gain_ref[k:k + 1]
    latents[...] = layer_norm(
        probes_ref[...].astype(jnp.float32), row_of[1:2]).astype(jnp.bfloat16).astype(jnp.float32)
    deep = wq_wide.shape[0]
    begin = pl.multiple_of(
        jnp.minimum(me * shard // LANES * LANES, channels - deep), LANES)
    wq_wide[pl.ds(pl.multiple_of(me * shard - begin, 8), shard)] = wq_ref[...].astype(jnp.float32)
    partial = jnp.dot(
        latents[:, pl.ds(begin, deep)].astype(jnp.bfloat16), wq_wide[...].astype(jnp.bfloat16),
        preferred_element_type=jnp.float32)
    for j in range(n):
        qpart[j // chips, j % chips] = partial[j * rows:(j + 1) * rows]
    hop(3, qpart.at[1 - core], qcore).start()

    def q_pair():
        hop(3, qpart.at[1 - core], qcore).wait()
        qpart[core] += qcore[...]
        qrecv[chip] = qpart[core, chip]
        share_start(0, lambda k: qpart.at[core, k], qrecv.at[chip])

    def q_sum():
        share_wait(0, qrecv.at[:chips - 1])
        qall[core, chip] = jnp.sum(qrecv[...], axis=0) * row_of[2:3]
        spread_start(1, qall)

    def q_hop():
        spread_hop(1, qall)

    def q_done():
        spread_wait(1, qall)
        for j in range(n):
            queries[j * rows:(j + 1) * rows] = qall[j // chips, j % chips]

    pairs = maps_ref.shape[0]
    frames = maps_ref.shape[2]
    high = act.shape[0] - 2
    half = act.shape[1] - 1
    group = filter_ref.shape[0] // 9
    tok_count = pairs * 2 * frames
    first_own = me * rows // 8 * 8

    act[0] = jnp.zeros(act.shape[1:], jnp.bfloat16)
    act[high + 1] = jnp.zeros(act.shape[1:], jnp.bfloat16)
    act[:, 0, 0] = jnp.zeros((high + 2, frames, channels), jnp.bfloat16)
    act[:, half, 1] = jnp.zeros((high + 2, frames, channels), jnp.bfloat16)
    own_rows = latents[pl.ds(pl.multiple_of(first_own, 8), 8)]
    source[tok_count:] = jnp.concatenate(
        [own_rows, jnp.zeros_like(own_rows)], axis=0).astype(jnp.bfloat16)
    q_pair()
    for t in range(1, AHEAD):
        send_own(t)
    taken[3].wait()

    def activate(i):
        g = jax.nn.gelu(maps_ref[i].astype(jnp.float32)).astype(jnp.bfloat16)
        y, p = i // half, lax.rem(i, half)
        act[y + 1, p, 1] = g[0]
        act[y + 1, p + 1, 0] = g[1]

    each(0, pairs, activate)
    taken[4].wait()
    taken[5].wait()
    for k in range(channels // LANES):
        row_of[0:1, k * LANES:(k + 1) * LANES] = gain_ref[k:k + 1]

    def convolve(c):
        lanes = pl.ds(pl.multiple_of(c * group, LANES), group)
        taps = jnp.concatenate([
            act[dy:dy + high, j // 2:j // 2 + half, j % 2, :, lanes].reshape(-1, group)
            for dy in range(3) for j in range(4)
        ], axis=1)
        none = jnp.zeros((group, group), jnp.bfloat16)

        def tap(dy, dx):
            if not 0 <= dx < 3:
                return none
            return filter_ref[(dy * 3 + dx) * group:(dy * 3 + dx + 1) * group, lanes]

        kernel = jnp.concatenate([
            jnp.concatenate([tap(dy, j), tap(dy, j - 1)], axis=1)
            for dy in range(3) for j in range(4)
        ], axis=0)
        both = jnp.dot(taps, kernel, preferred_element_type=jnp.float32)
        both = both.reshape(pairs, frames, 2 * group)
        summed[:, 0, :, lanes] = both[:, :, :group]
        summed[:, 1, :, lanes] = both[:, :, group:]

    def normalize(i):
        value = maps_ref[i].astype(jnp.float32) + RESIDUAL_SCALE * summed[i]
        value = layer_norm(value.reshape(2 * frames, channels), row_of[0:1])
        where = pl.multiple_of(i * 2 * frames, 16)
        source[pl.ds(where, 2 * frames)] = value.astype(jnp.bfloat16)

    parts = channels // group
    together = 5 if pairs % 5 == 0 else 1

    def normalize_some(i):
        for k in range(together):
            normalize(i * together + k)

    advance(0)
    each(0, parts // 2, convolve)
    taken[6].wait()
    hop(2, wo_ref.at[core], wo_ref.at[core]).start()
    advance(1)
    q_sum()
    each(parts // 2, parts, convolve)
    advance(2)
    each(0, pairs // together // 2, normalize_some)
    advance(3)
    each(pairs // together // 2, pairs // together, normalize_some)
    spread_wait(2, wo_ref)
    wo_wide[...] = jnp.zeros_like(wo_wide)
    for c in range(2):
        for head in range(heads):
            wo_wide[c, :, head * LANES:head * LANES + breadth] = (
                wo_ref[c, :, head * breadth:(head + 1) * breadth])
    q_hop()
    advance(4)
    q_done()

    per_block = heads // blocks
    lane = lax.broadcasted_iota(jnp.int32, (lats, LANES), 1)

    def weight(w, window_of):
        return jnp.concatenate(
            [gathered[w, j % 2, j // 2 % 2, j // 4, :, window_of] for j in range(n)], axis=0
        ).astype(jnp.bfloat16)

    def attend(first, early, between):
        block = slice(first * breadth, (first + per_block) * breadth)
        some = queries[:, block]
        at_lane = lax.broadcasted_iota(jnp.int32, some.shape, 1)
        asked = jnp.concatenate([
            jnp.where((at_lane >= i * breadth) & (at_lane < (i + 1) * breadth), some, 0.0)
            for i in range(per_block)
        ], axis=0)
        look = weight(0, block)
        raw = lax.dot_general(
            jnp.concatenate(halves(asked), axis=0), look, NT, preferred_element_type=jnp.float32)
        high, low = halves(raw[:per_block * lats] + raw[per_block * lats:])
        early()
        scores = lax.dot_general(high, source[...], NT, preferred_element_type=jnp.float32)
        scores += lax.dot_general(low, source[...], NT, preferred_element_type=jnp.float32)
        between()
        column = lax.broadcasted_iota(jnp.int32, scores.shape, 1)
        own = column - tok_count - (me * rows - first_own)
        live = (column < tok_count) | ((own >= 0) & (own < rows))
        scores = jnp.where(live, scores, -jnp.inf)
        row_max = jnp.max(scores, axis=1, keepdims=True)
        terms = jnp.exp(scores - row_max).astype(jnp.bfloat16)
        row_sum = jnp.sum(terms.astype(jnp.float32), axis=1, keepdims=True)
        mixed = jnp.dot(terms, source[...], preferred_element_type=jnp.float32)
        high, low = halves(mixed)
        u_high[first * lats:(first + per_block) * lats] = high
        u_low[first * lats:(first + per_block) * lats] = low
        for i in range(per_block):
            kept = jnp.zeros((lats, LANES), jnp.float32)
            spot = breadth
            for value in (row_max, row_sum):
                rest = value[i * lats:(i + 1) * lats]
                for _ in range(3):
                    top = rest.astype(jnp.bfloat16).astype(jnp.float32)
                    kept = jnp.where(lane == spot, top, kept)
                    rest = rest - top
                    spot += 1
            tail[first + i] = kept

    def project(first):
        for head in range(first, first + per_block):
            start, width = window(head, breadth)
            both = jnp.concatenate(
                [u_high[head * lats:(head + 1) * lats], u_low[head * lats:(head + 1) * lats]],
                axis=0)
            content = weight(1, slice(start, start + width))
            raw = jnp.dot(both, content, preferred_element_type=jnp.float32)
            raw = raw[:lats] + raw[lats:]
            shift = head * breadth - start
            if shift:
                raw = pltpu.roll(raw, width - shift, 1)
            raw = jnp.where(lane < breadth, raw[:, :LANES], tail[head])
            raw = raw.astype(jnp.bfloat16)
            for c in range(2):
                part[c, head * low_lats:(head + 1) * low_lats] = (
                    raw[c * low_lats:(c + 1) * low_lats])
            for k in range(head * low_lats // few, (head + 1) * low_lats // few):
                for c in range(2):
                    to_owner(k, c)

    def to_owner(k, c):
        own = part.at[c, k * few:(k + 1) * few]

        @pl.when(me != k * 2 + c)
        def _():
            remote(own, received.at[me], head_send.at[0], head_recv.at[0], k * 2 + c).start()

        @pl.when(me == k * 2 + c)
        def _():
            received[me] = part[c, k * few:(k + 1) * few]

    def ready(q, w):
        return w * chunks + -(-(q + 1) * per_block * breadth // cut) + 2

    step = 5
    for w in range(2):
        for q in range(blocks):
            while step <= ready(q, w):
                advance(step)
                step += 1
            if w == 0:
                attend(
                    q * per_block, lambda: advance_line(step), lambda: advance_rest(step))
                step += 1
            else:
                project(q * per_block)

    most = received.at[:n - 1]
    remote(most, most, head_send.at[0], head_recv.at[0], lax.rem(me + 1, n)).wait_recv()
    got = received[...].astype(jnp.float32)

    def number(spot):
        return got[:, :, spot:spot + 1] + got[:, :, spot + 1:spot + 2] + got[:, :, spot + 2:spot + 3]

    maxima = number(breadth)
    factor = jnp.exp(maxima - jnp.max(maxima, axis=0, keepdims=True))
    joint = jnp.sum(number(breadth + 3) * factor, axis=0)
    whole = jnp.sum(got * factor, axis=0) / joint
    narrow = lax.broadcasted_iota(jnp.int32, whole.shape, 1) < breadth
    att_all[chip] = jnp.where(narrow, whole, 0.0).astype(jnp.bfloat16)
    mine = att_all.at[chip]
    share_start(2, lambda k: mine, mine)
    share_wait(2, att_all.at[:chips - 1])
    pieces = low_lats // few if few < low_lats else 1
    heads_at = few // low_lats if few > low_lats else 1
    joined = []
    for head in range(heads):
        if few >= low_lats:
            first = head % heads_at * low_lats
            joined.append(att_all[head // heads_at, first:first + low_lats])
        else:
            joined.append(jnp.concatenate(
                [att_all[head * pieces + i] for i in range(pieces)], axis=0))
    joined = jnp.concatenate(joined, axis=1)
    wide = wo_ref.shape[1]
    for c in range(2):
        cols = lax.dot_general(joined, wo_wide[c], NT, preferred_element_type=jnp.float32)
        cols_all[core, chip, :, c * wide:(c + 1) * wide] = cols.astype(jnp.bfloat16)
    spread_start(4, cols_all)
    spread_hop(4, cols_all)
    spread_wait(4, cols_all)
    for c in range(2):
        for k in range(chips):
            attended_ref[c * low_lats:(c + 1) * low_lats, k * 2 * wide:(k + 1) * 2 * wide] = (
                cols_all[c, k])
    remote(most, most, head_send.at[0], head_recv.at[0], lax.rem(me + 1, n)).wait_send()
    finish_sends()


def per_device(
    n,
    picture_feature_maps,
    partitioned_filter_tensor,
    picture_token_layer_scaling,
    summary_probes,
    summary_probe_layer_scaling,
    asking_projection_tensor,
    lookup_projection_tensor,
    content_projection_tensor,
    final_projection_tensor,
    sharpness_coefficient,
):
    frames, high, across, channels = picture_feature_maps.shape
    heads = sharpness_coefficient.shape[0]
    lats = summary_probes.shape[0]
    maps = picture_feature_maps.transpose(1, 2, 0, 3)
    maps = maps.reshape(high * across // 2, 2, frames, channels)
    filters = partitioned_filter_tensor.reshape(-1, channels)
    tok_count = frames * high * across
    shard = asking_projection_tensor.shape[0]
    rows = lats // n
    extra = 16
    lookup, content = lookup_projection_tensor, content_projection_tensor
    wire = jnp.bfloat16 if shard % 16 == 0 else jnp.float32
    lookup, content = lookup.astype(wire), content.astype(wire)
    anywhere = pl.BlockSpec(memory_space=pl.ANY)
    vmem = pl.BlockSpec(memory_space=pltpu.VMEM)
    smem = pl.BlockSpec(memory_space=pltpu.SMEM)
    f32, bf16 = jnp.float32, jnp.bfloat16
    width = final_projection_tensor.shape[1]
    line = n // 4
    chips = n // 2
    chunks, blocks = 4, 4
    units = 2 * chunks
    few = lats * heads // n
    attended = pl.pallas_call(
        functools.partial(mixer, n, heads, chunks, blocks),
        out_shape=jax.ShapeDtypeStruct((lats, channels), bf16),
        in_specs=[anywhere] * 5 + [smem] + [anywhere] * 4,
        out_specs=vmem,
        scratch_shapes=[
            pltpu.VMEM(maps.shape, bf16),
            pltpu.VMEM(filters.shape, bf16),
            pltpu.VMEM((channels // LANES, LANES), f32),
            pltpu.VMEM((lats, channels), bf16),
            pltpu.VMEM((channels // LANES, LANES), f32),
            pltpu.VMEM((shard, channels), bf16),
            pltpu.VMEM((2, width, channels), bf16),
            pltpu.VMEM((8, channels), f32),
            pltpu.VMEM((lats, channels), f32),
            pltpu.VMEM((2 * LANES, channels), f32),
            pltpu.VMEM((2, 2, 2, line, shard, channels), wire),
            pltpu.VMEM((2, chips, rows, channels), f32),
            pltpu.VMEM((chips, rows, channels), f32),
            pltpu.VMEM((chips, rows, channels), f32),
            pltpu.VMEM((2, chips, rows, channels), f32),
            pltpu.VMEM((lats, channels), f32),
            pltpu.VMEM((tok_count + extra, channels), bf16),
            pltpu.VMEM((heads * lats, channels), bf16),
            pltpu.VMEM((heads * lats, channels), bf16),
            pltpu.VMEM((heads, lats, LANES), f32),
            pltpu.VMEM((2, heads * lats // 2, LANES), bf16),
            pltpu.VMEM((n, few, LANES), bf16),
            pltpu.VMEM((chips, few, LANES), bf16),
            pltpu.VMEM((2, chips, lats // 2, 2 * width), bf16),
            pltpu.VMEM((2, width, heads * LANES), bf16),
            pltpu.VMEM((high + 2, across // 2 + 1, 2, frames, channels), bf16),
            pltpu.VMEM((high * across // 2, 2, frames, channels), f32),
            pltpu.SemaphoreType.DMA((7,)),
            pltpu.SemaphoreType.DMA((2,)),
            pltpu.SemaphoreType.DMA((5,)),
            pltpu.SemaphoreType.DMA((units, line)),
            pltpu.SemaphoreType.DMA((units + 1,)),
            pltpu.SemaphoreType.DMA((units,)),
            pltpu.SemaphoreType.DMA((units,)),
            pltpu.SemaphoreType.DMA((units,)),
            pltpu.SemaphoreType.DMA((5,)),
            pltpu.SemaphoreType.DMA((5,)),
            pltpu.SemaphoreType.DMA((5,)),
            pltpu.SemaphoreType.DMA((5,)),
            pltpu.SemaphoreType.DMA((1,)),
            pltpu.SemaphoreType.DMA((1,)),
        ],
        compiler_params=pltpu.CompilerParams(
            collective_id=0, has_side_effects=True, vmem_limit_bytes=56 * 1024 * 1024
        ),
    )(
        maps, filters, picture_token_layer_scaling.reshape(-1, LANES), summary_probes,
        summary_probe_layer_scaling.reshape(-1, LANES), sharpness_coefficient,
        asking_projection_tensor, lookup, content, final_projection_tensor.T,
    ).astype(f32)
    return attended, (summary_probes.astype(f32) + attended).astype(bf16)


def solution(mesh):
    placed = (
        P(("groups", "wide"), None, None, None),
        P(),
        P(),
        P(),
        P(),
        P("wide", None),
        P("wide", None),
        P("wide", None),
        P(None, "wide"),
        P(),
    )
    return jax.shard_map(
        functools.partial(per_device, mesh.shape["wide"]),
        mesh=mesh,
        in_specs=placed,
        out_specs=(P("groups", None), P("groups", None)),
        check_vma=False,
    )
```
